32 devices in a mesh: member: 4 (over z), lon: 8 (over y, x, core).
Axes of the slice: x: 2, y: 2, z: 4, core: 2. Of those that a mesh axis runs over, the one named last changes fastest.
Arguments:
- latent: bfloat16 [8, 4, 360, 641], P('member', None, 'lon'), may hold values from -6 to 6
- member_seeds: int32 [8], P('member'), may hold values from 0 to 63
- member_table: bfloat16 [64, 641], replicated, may hold values from -6 to 6
- row_bands: int32 [4], replicated, may hold values from 0 to 15
- disco_basis: bfloat16 [16, 4, 7, 7], replicated, may hold values from -0.8984375 to 0.8984375
- w_disco: bfloat16 [2564, 641], replicated, may hold values from -0.125 to 0.125
- w_expand: bfloat16 [641, 1282], replicated, may hold values from -0.25 to 0.25
- w_reduce: bfloat16 [1282, 641], replicated, may hold values from -0.15625 to 0.15625
- w_decode: bfloat16 [641, 288], replicated, may hold values from -0.25 to 0.25
- target: bfloat16 [4, 360, 288], P(None, 'lon'), may hold values from -12 to 12
Outputs:
- latent_grad: bfloat16 [8, 4, 360, 641], P('member', None, 'lon')
- grad_disco: bfloat16 [2564, 641], replicated
- grad_expand: bfloat16 [641, 1282], replicated
- grad_reduce: bfloat16 [1282, 641], replicated
- grad_decode: bfloat16 [641, 288], replicated
The draws below stay inside these ranges and needn't reach their ends.
All inputs are finite; a program needn't handle non-finite values.
Results may differ from the reference program's by a relative error of at most 0.025.
Values may be sent and summed in bfloat16 or wider, within the bound.
No kernel may reach another device: no remote copies, remote signals or barrier semaphores. Data moves between devices by JAX's collectives and lax.ppermute only.
A program may use at most 128 MiB of HBM per device.

```python
import math
import jax
import jax.numpy as jnp
from jax import lax

CH = 641
HID = 1282
OUTC = 288
BASES = 4
BANDS = 16
SEEDS = 64
ROWS = 4
MEMBERS = 8
LON = 360


def touch_ends(values, own_key, low, largest):
    extent = values.shape
    index_at = [jax.random.randint(jax.random.fold_in(own_key, axis), (), 0, extent[axis]) for axis in range(len(extent))]
    values = values.at[tuple(index_at)].set(low)
    longest = extent.index(max(extent))
    index_at[longest] = (index_at[longest] + 1) % extent[longest]
    return values.at[tuple(index_at)].set(largest)


def block_levels(key, extent, pieces, low, largest):
    level = 1.0
    for dim, shards_of in pieces:
        steps = jax.random.uniform(jax.random.fold_in(jax.random.fold_in(key, 6), dim), (shards_of,), jnp.float32, low / len(pieces), largest / len(pieces))
        level = level * jnp.repeat(jnp.exp(steps), extent[dim] // shards_of).reshape((-1,) + (1,) * (len(extent) - 1 - dim))
    return level


def noise(own_key, extent, scale, limit, shards=(), dtype=jnp.bfloat16):
    array = scale * jax.random.normal(own_key, extent, jnp.float32)
    if shards:
        array = array * block_levels(own_key, extent, shards, -0.22, 0.18)
    return jnp.clip(array, -limit, limit).astype(dtype)


def setup_inputs(seed: int = 0) -> dict:
    keys = jax.random.split(jax.random.key(seed), 11)
    latent = noise(keys[0], (MEMBERS, ROWS, LON, CH), 1.0, 6.0, ((0, 4), (2, 8)))
    member_seeds = touch_ends(jax.random.randint(keys[1], (MEMBERS,), 0, SEEDS), jax.random.fold_in(keys[1], 1), 0, SEEDS - 1).astype(jnp.int32)
    member_table = noise(keys[2], (SEEDS, CH), 1.0, 6.0)
    row_bands = touch_ends(jax.random.randint(keys[3], (ROWS,), 0, BANDS), jax.random.fold_in(keys[3], 1), 0, BANDS - 1).astype(jnp.int32)
    disco_basis = noise(keys[4], (BANDS, BASES, 7, 7), 0.15, 0.8984375)
    w_disco = noise(keys[5], (BASES * CH, CH), (BASES * CH) ** -0.5, 0.125)
    w_expand = noise(keys[6], (CH, HID), CH ** -0.5, 0.25)
    w_reduce = noise(keys[7], (HID, CH), HID ** -0.5, 0.15625)
    w_decode = noise(keys[8], (CH, OUTC), CH ** -0.5, 0.25)
    target = noise(keys[9], (ROWS, LON, OUTC), 2.0, 12.0, ((1, 8),))
    return dict(latent=latent, member_seeds=member_seeds, member_table=member_table, row_bands=row_bands, disco_basis=disco_basis, w_disco=w_disco, w_expand=w_expand, w_reduce=w_reduce, w_decode=w_decode, target=target)


stencil_reach = 3
smooth = 0.5

def smooth_slope(difference):
    return difference / jnp.sqrt(difference * difference + smooth * smooth)

def gelu_value(value):
    return jax.nn.gelu(value, approximate=True)

def wrap_lon(field):
    return jnp.concatenate([field[:, -stencil_reach:], field, field[:, :stencil_reach]], axis=1)

def spread_member(field, stencil):
    row_count = field.shape[0]
    lon_count = field.shape[1]
    widened = wrap_lon(field)
    padded = jnp.pad(widened, ((stencil_reach, stencil_reach), (0, 0), (0, 0)))
    summed = None
    for tap_row in range(7):
        band_rows = padded[tap_row:tap_row + row_count].astype(jnp.float32)
        window = jnp.stack([band_rows[:, tap_col:tap_col + lon_count] for tap_col in range(7)], axis=2)
        contrib = jnp.einsum('rwbc,rkb->rwkc', window, stencil[:, :, tap_row, :].astype(jnp.float32))
        summed = contrib if summed is None else summed + contrib
    out_shape = summed.shape
    return summed.astype(jnp.bfloat16).reshape(out_shape[0], out_shape[1], out_shape[2] * out_shape[3])

def collect_member(grad, stencil):
    row_count = grad.shape[0]
    lon_count = grad.shape[1]
    basis_count = stencil.shape[1]
    split = grad.reshape(row_count, lon_count, basis_count, grad.shape[2] // basis_count)
    widened = wrap_lon(split)
    padded = jnp.pad(widened, ((3, 3), (0, 0), (0, 0), (0, 0)))
    stencil_tall = jnp.pad(stencil, ((3, 3), (0, 0), (0, 0), (0, 0)))
    summed = None
    for tap_row in range(7):
        source = padded[6 - tap_row:6 - tap_row + row_count].astype(jnp.float32)
        tap_coef = stencil_tall[6 - tap_row:6 - tap_row + row_count, :, tap_row, :].astype(jnp.float32)
        window = jnp.stack([source[:, 6 - tap_col:6 - tap_col + lon_count] for tap_col in range(7)], axis=2)
        contrib = jnp.einsum('rwbkc,rkb->rwc', window, tap_coef)
        summed = contrib if summed is None else summed + contrib
    return summed

def reference(latent, member_seeds, member_table, row_bands, disco_basis, w_disco, w_expand, w_reduce, w_decode, target):
    member_count, row_count, lon_count, chan_count = latent.shape
    stencil = disco_basis[row_bands]
    offsets = member_table[member_seeds].astype(jnp.float32)
    seeded = (latent.astype(jnp.float32) + offsets[:, None, None, :]).astype(jnp.bfloat16)
    spread = lax.map(lambda field: spread_member(field, stencil), seeded)
    flat_rows = member_count * row_count * lon_count
    spread_rows = spread.reshape(flat_rows, -1)
    seeded_rows = seeded.reshape(flat_rows, chan_count)
    conv_out = jnp.dot(spread_rows, w_disco, preferred_element_type=jnp.float32)
    hidden_in = (seeded_rows.astype(jnp.float32) + conv_out).astype(jnp.bfloat16)
    pre_act = jnp.dot(hidden_in, w_expand, preferred_element_type=jnp.float32)
    gelu_out = gelu_value(pre_act).astype(jnp.bfloat16)
    mixed = (hidden_in.astype(jnp.float32) + jnp.dot(gelu_out, w_reduce, preferred_element_type=jnp.float32)).astype(jnp.bfloat16)
    fields = jnp.dot(mixed, w_decode, preferred_element_type=jnp.float32).astype(jnp.bfloat16)
    fields = fields.reshape(member_count, row_count, lon_count, -1).astype(jnp.float32)
    paired = jnp.zeros_like(fields)
    for other in range(member_count):
        paired = paired + smooth_slope(fields - fields[other][None])
    field_grad = (smooth_slope(fields - target.astype(jnp.float32)[None]) - paired / (member_count - 1)).astype(jnp.bfloat16)
    grad_rows = field_grad.reshape(flat_rows, -1)
    mixed_grad = jnp.dot(grad_rows, w_decode.T, preferred_element_type=jnp.float32).astype(jnp.bfloat16)
    gelu_grad = jnp.dot(mixed_grad, w_reduce.T, preferred_element_type=jnp.float32)
    unused, pullback = jax.vjp(gelu_value, pre_act)
    pre_grad = pullback(gelu_grad)[0].astype(jnp.bfloat16)
    hidden_grad = (mixed_grad.astype(jnp.float32) + jnp.dot(pre_grad, w_expand.T, preferred_element_type=jnp.float32)).astype(jnp.bfloat16)
    spread_grad = jnp.dot(hidden_grad, w_disco.T, preferred_element_type=jnp.float32).astype(jnp.bfloat16)
    spread_grad = spread_grad.reshape(member_count, row_count, lon_count, -1)
    carried = lax.map(lambda grad: collect_member(grad, stencil), spread_grad)
    latent_grad = (hidden_grad.astype(jnp.float32).reshape(member_count, row_count, lon_count, chan_count) + carried).astype(jnp.bfloat16)
    factor = 1.0 / math.sqrt(member_count * row_count * lon_count)
    grad_disco = (jnp.dot(spread_rows.T, hidden_grad, preferred_element_type=jnp.float32) * factor).astype(jnp.bfloat16)
    grad_expand = (jnp.dot(hidden_in.T, pre_grad, preferred_element_type=jnp.float32) * factor).astype(jnp.bfloat16)
    grad_reduce = (jnp.dot(gelu_out.T, mixed_grad, preferred_element_type=jnp.float32) * factor).astype(jnp.bfloat16)
    grad_decode = (jnp.dot(mixed.T, grad_rows, preferred_element_type=jnp.float32) * factor).astype(jnp.bfloat16)
    return (latent_grad, grad_disco, grad_expand, grad_reduce, grad_decode)
```

```python
import functools
import math

import jax
import jax.numpy as jnp
from jax import lax
from jax.experimental import pallas as pl
from jax.experimental.pallas import tpu as pltpu
from jax.sharding import PartitionSpec as P

reach = 3
taps = 2 * reach + 1
smooth = 0.5
LANES = 128
TILE = 16
VMEM_LIMIT = 56 * 2**20
F32 = jnp.float32
BF16 = jnp.bfloat16


def up(value, unit):
    return -(-value // unit) * unit


def dot(a, b, ca=1, cb=0):
    return lax.dot_general(a, b, (((ca,), (cb,)), ((), ())), preferred_element_type=F32)


def slope(d):
    return d * lax.rsqrt(d * d + smooth * smooth)


def vmem_call(body, outs, args, smem=0, scratch=(), name=None):
    specs = [pl.BlockSpec(memory_space=pltpu.SMEM)] * smem
    specs += [pl.BlockSpec(memory_space=pltpu.VMEM)] * (len(args) - smem)
    return pl.pallas_call(
        body,
        out_shape=[jax.ShapeDtypeStruct(shape, dtype) for shape, dtype in outs],
        in_specs=specs,
        out_specs=[pl.BlockSpec(memory_space=pltpu.VMEM)] * len(outs),
        scratch_shapes=list(scratch),
        compiler_params=pltpu.CompilerParams(vmem_limit_bytes=VMEM_LIMIT),
        name=name,
    )(*args)


def forward_body(
    dims, seeds, bands, basis, latent, left, right, table, w_disco, w_expand, w_reduce, w_decode,
    stencil_out, spread_out, hidden_out, gelu_out, slope_out, mixed_out, fields_out, wide,
):
    members, rows, lons, chans, lon_pad, slot, bases, piece, share = dims
    chan_pad = up(chans, LANES)
    points = rows * lon_pad
    per_tile = LANES // slot
    lane = lax.broadcasted_iota(jnp.int32, (lon_pad, LANES), 1)
    lon = lax.broadcasted_iota(jnp.int32, (lon_pad, LANES), 0)
    place = lane % slot
    own = place < lons
    before = (place >= lon_pad) & (place < lon_pad + reach)
    after = (place >= lon_pad + 8) & (place < lon_pad + 8 + reach)
    wide_lon = jnp.where(own, place + reach, jnp.where(before, place - lon_pad, place - lon_pad - 8 + lons + reach))
    tap = jnp.where((own | before | after) & (lon < lons), wide_lon - lon, -1)
    tap = jnp.where(lane < slot, tap, tap + 1000 * (lane // slot))
    masks = [[tap == 1000 * part + b for b in range(taps)] for part in range(per_tile)]
    for r in range(rows):
        band = bands[r]
        for k in range(bases):
            for t in range(rows // per_tile):
                block = jnp.zeros((lon_pad, LANES), F32)
                for part in range(per_tile):
                    a = t * per_tile + part - r + reach
                    if not 0 <= a < taps:
                        continue
                    base = ((band * bases + k) * taps + a) * taps
                    for b in range(taps):
                        block = jnp.where(masks[part][b], basis[base + b], block)
                stencil_out[k * points + r * lon_pad : k * points + (r + 1) * lon_pad, t * LANES : (t + 1) * LANES] = block.astype(BF16)
    seed_count = table.shape[0]
    mrow = lax.broadcasted_iota(jnp.int32, (TILE, seed_count), 0)
    mcol = lax.broadcasted_iota(jnp.int32, (TILE, seed_count), 1)
    onehot = jnp.zeros((TILE, seed_count), F32)
    for m in range(members):
        onehot = jnp.where((mrow == m) & (mcol == seeds[m]), 1.0, onehot)
    offsets = dot(onehot.astype(BF16), table[...])
    wide[...] = jnp.zeros_like(wide)
    for m in range(members):
        off = offsets[m : m + 1, :]
        for r in range(rows):
            for ref, start, count in ((latent, 0, lons), (left, lon_pad, reach), (right, lon_pad + 8, reach)):
                seeded = (ref[m, r].astype(F32) + off).astype(BF16).astype(F32)
                wide[m, r * slot + start : r * slot + start + count, :chans] = seeded
    for m in range(members):
        full = wide[m]
        carry = None
        for k in range(bases):
            moved = full if k == 0 else pltpu.roll(full, k, 1)
            out = dot(stencil_out[k * points : (k + 1) * points, :], moved.astype(BF16))
            width = chan_pad - LANES
            first = out[:, :LANES] if carry is None else out[:, :LANES] + carry
            rows_here = slice(m * points, (m + 1) * points)
            spread_out[rows_here, k * width : k * width + LANES] = first.astype(BF16)
            spread_out[rows_here, k * width + LANES : (k + 1) * width] = out[:, LANES:width].astype(BF16)
            carry = out[:, width:]
        spread_out[rows_here, bases * width : bases * width + LANES] = carry.astype(BF16)
    seeded_rows = jnp.concatenate(
        [wide[m, r * slot : r * slot + lon_pad, :chans] for m in range(members) for r in range(rows)], axis=0
    )
    conv = dot(spread_out[:, : bases * chans], w_disco[...])
    hidden = (seeded_rows + conv).astype(BF16)
    hidden_out[...] = hidden
    pre = dot(hidden, w_expand[...])
    rate = math.sqrt(2.0 / math.pi)
    square = pre * pre
    th = jnp.tanh(rate * (pre + 0.044715 * (square * pre)))
    half = 0.5 * (1.0 + th)
    act = (pre * half).astype(BF16)
    gelu_out[...] = act
    slope_out[...] = (half + 0.5 * pre * (1.0 - th * th) * (rate * (1.0 + 3 * 0.044715 * square))).astype(BF16)
    mixed = (hidden.astype(F32) + dot(act, w_reduce[...])).astype(BF16)
    mixed_out[...] = mixed
    fields = dot(mixed, w_decode[...])
    outs = fields.shape[1]
    turned = jnp.swapaxes(jnp.pad(fields, ((0, 0), (0, up(outs, LANES) - outs))), 0, 1)
    for q in range(share):
        low, high = q * piece, min((q + 1) * piece, up(outs, TILE))
        if high > low:
            fields_out[q, : high - low, :] = turned[low:high].astype(BF16)
        if high < (q + 1) * piece:
            start = max(high - low, 0)
            fields_out[q, start:, :] = jnp.zeros((piece - start, turned.shape[1]), BF16)


def crps_body(count, points, members, total, *refs):
    fields = [ref[...].astype(F32) for ref in refs[:count]]
    observed = refs[count][...].astype(F32)
    outs = refs[count + 1 :]
    turned = [[f] + [pltpu.roll(f, t * points, 1) for t in range(1, members)] for f in fields]
    for i in range(count):
        paired = jnp.zeros_like(observed)
        for j in range(count):
            for t in range(members):
                if i == j and t == 0:
                    continue
                paired = paired + slope(fields[i] - turned[j][t])
        outs[i][...] = (slope(fields[i] - observed) - paired * (1.0 / (total - 1))).astype(BF16)


def last_rows(values, col, height=TILE):
    tail = values[:, col:]
    extra = LANES - tail.shape[1]
    if extra:
        tail = jnp.concatenate([tail, jnp.zeros((tail.shape[0], extra), tail.dtype)], axis=1)
    return jnp.swapaxes(tail.astype(F32), 0, 1)[:height].astype(BF16)


def fold_rows(rows, width, first, into):
    n = rows.shape[1]
    count = -(-n // width)
    if count * width > n:
        rows = jnp.concatenate([rows, jnp.zeros((1, count * width - n), rows.dtype)], axis=1)
    at = lax.broadcasted_iota(jnp.int32, into.shape, 0)
    for t in range(count):
        into = jnp.where(at == first + t, rows[:, t * width : (t + 1) * width], into)
    return into, first + count


def backward_body(
    dims, scale, me, *refs,
):
    share, piece, outs, chans, hidden_units, width = dims
    grads = refs[:share]
    (w_decode, w_reduce, w_expand, slopes, hidden, gelu, mixed, packed, hidden_grad_out, turned_grad) = refs[share:]
    for d in range(share):
        turned_grad[pl.ds(pl.multiple_of(lax.rem(me[0] + d, share) * piece, TILE), piece), :] = grads[d][...]
    field_t = turned_grad[: up(outs, TILE)]
    field = jnp.swapaxes(field_t.astype(F32), 0, 1).astype(BF16)[:, :outs]
    mixed_grad = dot(field, w_decode[...], 1, 1).astype(BF16)
    gelu_grad = dot(mixed_grad, w_reduce[...], 1, 1)
    pre_grad = (gelu_grad * slopes[...].astype(F32)).astype(BF16)
    hidden_grad = (mixed_grad.astype(F32) + dot(pre_grad, w_expand[...], 1, 1)).astype(BF16)
    hidden_grad_out[...] = hidden_grad
    row = 0
    misc = jnp.zeros((TILE, width), F32)
    packed[row : row + hidden_units, :] = (dot(gelu[...], mixed_grad[:, :width], 0, 0) * scale).astype(BF16)
    tail = dot(last_rows(mixed_grad, width), gelu[...])
    misc, at = fold_rows(tail[0:1], width, 0, misc)
    row += up(hidden_units, TILE)
    for part in range(hidden_units // width):
        packed[row : row + chans, :] = (dot(hidden[...], pre_grad[:, part * width : (part + 1) * width], 0, 0) * scale).astype(BF16)
        row += up(chans, TILE)
    rest = hidden_units // width * width
    tail = dot(last_rows(pre_grad, rest), hidden[...])
    for i in range(hidden_units - rest):
        misc, at = fold_rows(tail[i : i + 1], width, at, misc)
    packed[row : row + outs, :] = (dot(field_t[:outs], mixed[:, :width]) * scale).astype(BF16)
    row += up(outs, TILE)
    tail = dot(last_rows(mixed[...], width), field)
    misc, at = fold_rows(tail[0:1], width, at, misc)
    packed[row : row + TILE, :] = (misc * scale).astype(BF16)
    if packed.shape[0] > row + TILE:
        packed[row + TILE :, :] = jnp.zeros((packed.shape[0] - row - TILE, width), BF16)


def disco_body(scale, width, tall, spread, hidden_grad, packed):
    grad = hidden_grad[...]
    value = dot(spread[...], grad[:, :width], 0, 0)
    packed[:tall, :] = (value[:tall] * scale).astype(BF16)
    tail = dot(last_rows(grad, width), spread[...])
    misc, at = fold_rows(tail[0:1, :tall], width, 0, jnp.zeros((TILE, width), F32))
    packed[tall : tall + TILE, :] = (misc * scale).astype(BF16)
    if packed.shape[0] > tall + TILE:
        packed[tall + TILE :, :] = jnp.zeros((packed.shape[0] - tall - TILE, width), BF16)


def collect_body(dims, hidden_grad, w_disco, stencil, out, left_out, right_out):
    members, rows, lons, chans, lon_pad, slot, bases = dims
    chan_pad = up(chans, LANES)
    points = rows * lon_pad
    width = chan_pad - LANES
    full = bases * width + LANES
    grad = dot(hidden_grad[...], w_disco[...], 1, 1).astype(BF16)
    grad = jnp.concatenate([grad, jnp.zeros((grad.shape[0], full - grad.shape[1]), BF16)], axis=1)
    for m in range(members):
        total = None
        for k in range(bases):
            part = dot(stencil[k * points : (k + 1) * points, :], grad[m * points : (m + 1) * points, k * width : k * width + chan_pad], 0, 0)
            part = part if k == 0 else pltpu.roll(part, chan_pad - k, 1)
            total = part if total is None else total + part
        for r in range(rows):
            at = r * slot
            own = hidden_grad[m * points + r * lon_pad : m * points + (r + 1) * lon_pad, :].astype(F32)
            out[m, r] = (own + total[at : at + lon_pad, :chans])[:lons]
            left_out[m, r] = total[at + lon_pad : at + lon_pad + 8, :chans][:reach]
            right_out[m, r] = total[at + lon_pad + 8 : at + lon_pad + 16, :chans][:reach]


def bits_of(axis):
    size, out, bit = lax.axis_size(axis), [], 1
    while bit < size:
        out.append((axis, bit))
        bit *= 2
    return out


def swap(x, pair):
    members, lons = lax.axis_size("member"), lax.axis_size("lon")
    perm = []
    for m in range(members):
        for n in range(lons):
            axis, bit = pair[n % 2]
            to = (m ^ bit) * lons + n if axis == "member" else m * lons + (n ^ bit)
            perm.append((m * lons + n, to))
    return lax.ppermute(x, ("member", "lon"), perm)


def my_bit(pair):
    bits = [lax.axis_index(axis) // bit % 2 for axis, bit in pair]
    return jnp.where(lax.axis_index("lon") % 2 == 0, bits[0], bits[1])


def add_rounded(a, b):
    return (a.astype(F32) + b.astype(F32)).astype(BF16)


def pick(state, start, count):
    kept, offset, got, got_offset = state
    mine = lax.dynamic_slice_in_dim(kept, offset + start, count, axis=0)
    return add_rounded(mine, lax.dynamic_slice_in_dim(got, got_offset + start, count, axis=0))


def streams():
    core, *lon = bits_of("lon")
    mem = bits_of("member")
    first = [(d, d) for d in lon + mem]
    second = [(d, d) for d in lon[1:] + mem[:1] + lon[:1] + mem[1:]]
    third = [(d, d) for d in mem[:1] + lon + mem[1:]]
    return (core, core), [first, second, third]


def row_unit():
    core, orders = streams()
    return 2 * 8 * 2 ** (len(orders[0]) - 1)


def all_sum(x, shares=(3, 3, 2)):
    core, orders = streams()
    count = x.shape[0] // 2
    bit = my_bit(core)
    got = swap(lax.dynamic_slice_in_dim(x, (1 - bit) * count, count, axis=0), core)
    unit = row_unit() // 2
    units = count // unit
    sizes = [units * s // sum(shares) * unit for s in shares[1:]]
    sizes = [count - sum(sizes)] + sizes
    steps = len(orders[0])
    lanes = range(len(orders))
    offsets = [sum(sizes[:i]) for i in lanes]
    states = [(x, bit * count + offsets[i], got, offsets[i]) for i in lanes]
    rows, trail = list(sizes), []
    for s in range(steps - 1):
        rows = [r // 2 for r in rows]
        sides = [my_bit(orders[i][s]) for i in lanes]
        gots = [swap(pick(states[i], (1 - sides[i]) * rows[i], rows[i]), orders[i][s]) for i in lanes]
        states = [(pick(states[i], sides[i] * rows[i], rows[i]), 0, gots[i], 0) for i in lanes]
        trail.append(sides)
    mine = [pick(states[i], 0, rows[i]) for i in lanes]
    outs = [add_rounded(mine[i], swap(mine[i], orders[i][-1])) for i in lanes]
    for s in range(steps - 2, -1, -1):
        gots = [swap(outs[i], orders[i][s]) for i in lanes]
        first = [trail[s][i] == 0 for i in lanes]
        outs = [
            jnp.concatenate([jnp.where(f, o, g), jnp.where(f, g, o)], axis=0)
            for f, o, g in zip(first, outs, gots)
        ]
    others = [swap(o, core) for o in outs]
    return jnp.concatenate([jnp.where(bit == side, o, q) for side in (0, 1) for o, q in zip(outs, others)], axis=0)


def shifted(x, axis, by):
    size = lax.axis_size(axis)
    return lax.ppermute(x, axis, [(i, (i + by) % size) for i in range(size)])


def spread_out(piece_of, axis):
    size = lax.axis_size(axis)
    return [piece_of(0)] + [shifted(piece_of(size - d), axis, -d) for d in range(1, size)]


def per_device(
    latent, member_seeds, member_table, row_bands, disco_basis, w_disco, w_expand, w_reduce, w_decode, target
):
    members, rows, lons, chans = latent.shape
    bases = disco_basis.shape[1]
    hidden_units = w_expand.shape[1]
    outs = w_decode.shape[1]
    share = lax.axis_size("member")
    total_members = members * share
    lon_pad = up(lons, TILE)
    slot = lon_pad + TILE
    points = rows * lon_pad
    flat = members * points
    width = chans // LANES * LANES
    full = bases * width + LANES
    piece = TILE * -(-up(outs, TILE) // (TILE * share))
    me = lax.axis_index("member")
    left = shifted(latent[:, :, lons - reach :], "lon", 1)
    right = shifted(latent[:, :, :reach], "lon", -1)
    dims = (members, rows, lons, chans, lon_pad, slot, bases, piece, share)
    stencil, spread, hidden, gelu, slopes, mixed, fields = vmem_call(
        functools.partial(forward_body, dims),
        [
            ((bases * points, rows * slot), BF16),
            ((flat, full), BF16),
            ((flat, chans), BF16),
            ((flat, hidden_units), BF16),
            ((flat, hidden_units), BF16),
            ((flat, chans), BF16),
            ((share, piece, flat), BF16),
        ],
        [
            member_seeds, row_bands, disco_basis.astype(F32).reshape(-1),
            latent, left, right, member_table, w_disco, w_expand, w_reduce, w_decode,
        ],
        smem=3,
        scratch=[pltpu.VMEM((members, rows * slot, up(chans, LANES)), F32)],
        name="forward",
    )
    observed = jnp.pad(target, ((0, 0), (0, lon_pad - lons), (0, share * piece - outs))).reshape(points, share * piece).T
    observed = jnp.concatenate([observed] * members, axis=1)
    observed = lax.dynamic_slice_in_dim(observed, me * piece, piece, axis=0)
    here = spread_out(lambda d: lax.dynamic_index_in_dim(fields, (me + d) % share, 0, keepdims=False), "member")
    grads = vmem_call(
        functools.partial(crps_body, share, points, members, total_members),
        [((piece, flat), BF16)] * share,
        here + [observed],
        name="crps",
    )
    back = spread_out(lambda d: grads[d], "member")
    scale = 1.0 / math.sqrt(total_members * rows * lons * lax.axis_size("lon"))
    unit = row_unit()
    height = up(hidden_units, TILE) + hidden_units // width * up(chans, TILE) + up(outs, TILE) + TILE
    packed, hidden_grad = vmem_call(
        functools.partial(backward_body, (share, piece, outs, chans, hidden_units, width), scale),
        [((up(height, unit), width), BF16), ((flat, chans), BF16)],
        [me.astype(jnp.int32).reshape(1)] + back + [w_decode, w_reduce, w_expand, slopes, hidden, gelu, mixed],
        smem=1,
        scratch=[pltpu.VMEM((share * piece, flat), BF16)],
        name="backward",
    )
    tall = up(bases * chans, TILE)
    (packed_disco,) = vmem_call(
        functools.partial(disco_body, scale, width, tall),
        [((up(tall + TILE, unit), width), BF16)],
        [spread, hidden_grad],
        name="disco",
    )
    summed = all_sum(packed)
    summed_disco = all_sum(packed_disco)
    dims = (members, rows, lons, chans, lon_pad, slot, bases)
    latent_grad, to_left, to_right = vmem_call(
        functools.partial(collect_body, dims),
        [(latent.shape, F32), ((members, rows, reach, chans), F32), ((members, rows, reach, chans), F32)],
        [hidden_grad, w_disco, stencil],
        name="collect",
    )
    from_right = shifted(to_left, "lon", -1)
    from_left = shifted(to_right, "lon", 1)
    edge = [(0, 0, 0)] * 2
    latent_grad = (
        latent_grad
        + lax.pad(from_right, jnp.float32(0), edge + [(lons - reach, 0, 0), (0, 0, 0)])
        + lax.pad(from_left, jnp.float32(0), edge + [(0, lons - reach, 0), (0, 0, 0)])
    ).astype(BF16)

    def column(block, first, count):
        wide = -(-count // width)
        return block[first : first + wide].reshape(-1)[:count]

    disco_col = column(summed_disco, tall, bases * chans)
    grad_disco = jnp.concatenate([summed_disco[: bases * chans], disco_col[:, None]], axis=1)
    row = 0
    misc = height - TILE
    grad_reduce = jnp.concatenate([summed[:hidden_units], column(summed, misc, hidden_units)[:, None]], axis=1)
    misc += -(-hidden_units // width)
    row += up(hidden_units, TILE)
    parts = []
    for part in range(hidden_units // width):
        parts.append(summed[row : row + chans])
        row += up(chans, TILE)
    for i in range(hidden_units - hidden_units // width * width):
        parts.append(column(summed, misc, chans)[:, None])
        misc += -(-chans // width)
    grad_expand = jnp.concatenate(parts, axis=1)
    grad_decode = jnp.concatenate([summed[row : row + outs].T, column(summed, misc, outs)[None]], axis=0)
    return latent_grad, grad_disco, grad_expand, grad_reduce, grad_decode


def solution(mesh):
    placed = (
        P("member", None, "lon", None),
        P("member"),
        P(),
        P(),
        P(),
        P(),
        P(),
        P(),
        P(),
        P(None, "lon", None),
    )
    return jax.shard_map(
        per_device,
        mesh=mesh,
        in_specs=placed,
        out_specs=(P("member", None, "lon", None), P(), P(), P(), P()),
        check_vma=False,
    )
```

```python
import functools
import math

import jax
import jax.numpy as jnp
from jax import lax
from jax.experimental import pallas as pl
from jax.experimental.pallas import tpu as pltpu
from jax.sharding import PartitionSpec as P

reach = 3
taps = 2 * reach + 1
smooth = 0.5
LANES = 128
TILE = 16
VMEM_LIMIT = 56 * 2**20
F32 = jnp.float32
BF16 = jnp.bfloat16


def up(value, unit):
    return -(-value // unit) * unit


def dot(a, b, ca=1, cb=0):
    return lax.dot_general(a, b, (((ca,), (cb,)), ((), ())), preferred_element_type=F32)


def slope(d):
    return d * lax.rsqrt(d * d + smooth * smooth)


def vmem_call(body, outs, args, smem=0, scratch=(), name=None):
    specs = [pl.BlockSpec(memory_space=pltpu.SMEM)] * smem
    specs += [pl.BlockSpec(memory_space=pltpu.VMEM)] * (len(args) - smem)
    return pl.pallas_call(
        body,
        out_shape=[jax.ShapeDtypeStruct(shape, dtype) for shape, dtype in outs],
        in_specs=specs,
        out_specs=[pl.BlockSpec(memory_space=pltpu.VMEM)] * len(outs),
        scratch_shapes=list(scratch),
        compiler_params=pltpu.CompilerParams(vmem_limit_bytes=VMEM_LIMIT),
        cost_estimate=pl.CostEstimate(flops=0, bytes_accessed=0, transcendentals=0),
        name=name,
    )(*args)


def forward_body(
    dims, seeds, bands, basis, latent, left, right, table, w_disco, w_expand, w_reduce, w_decode,
    stencil_out, spread_out, hidden_out, gelu_out, slope_out, mixed_out, fields_out, wide,
):
    members, rows, lons, chans, lon_pad, slot, bases, piece, share = dims
    chan_pad = up(chans, LANES)
    points = rows * lon_pad
    per_tile = LANES // slot
    lane = lax.broadcasted_iota(jnp.int32, (lon_pad, LANES), 1)
    lon = lax.broadcasted_iota(jnp.int32, (lon_pad, LANES), 0)
    place = lane % slot
    own = place < lons
    before = (place >= lon_pad) & (place < lon_pad + reach)
    after = (place >= lon_pad + 8) & (place < lon_pad + 8 + reach)
    wide_lon = jnp.where(own, place + reach, jnp.where(before, place - lon_pad, place - lon_pad - 8 + lons + reach))
    tap = jnp.where((own | before | after) & (lon < lons), wide_lon - lon, -1)
    tap = jnp.where(lane < slot, tap, tap + 1000 * (lane // slot))
    masks = [[tap == 1000 * part + b for b in range(taps)] for part in range(per_tile)]
    for r in range(rows):
        band = bands[r]
        for k in range(bases):
            for t in range(rows // per_tile):
                block = jnp.zeros((lon_pad, LANES), F32)
                for part in range(per_tile):
                    a = t * per_tile + part - r + reach
                    if not 0 <= a < taps:
                        continue
                    base = ((band * bases + k) * taps + a) * taps
                    for b in range(taps):
                        block = jnp.where(masks[part][b], basis[base + b], block)
                stencil_out[k * points + r * lon_pad : k * points + (r + 1) * lon_pad, t * LANES : (t + 1) * LANES] = block.astype(BF16)
    seed_count = table.shape[0]
    mrow = lax.broadcasted_iota(jnp.int32, (TILE, seed_count), 0)
    mcol = lax.broadcasted_iota(jnp.int32, (TILE, seed_count), 1)
    onehot = jnp.zeros((TILE, seed_count), F32)
    for m in range(members):
        onehot = jnp.where((mrow == m) & (mcol == seeds[m]), 1.0, onehot)
    offsets = dot(onehot.astype(BF16), table[...])
    wide[...] = jnp.zeros_like(wide)
    for m in range(members):
        off = offsets[m : m + 1, :]
        for r in range(rows):
            for ref, start, count in ((latent, 0, lons), (left, lon_pad, reach), (right, lon_pad + 8, reach)):
                seeded = (ref[m, r].astype(F32) + off).astype(BF16).astype(F32)
                wide[m, r * slot + start : r * slot + start + count, :chans] = seeded
    for m in range(members):
        full = wide[m]
        carry = None
        for k in range(bases):
            moved = full if k == 0 else pltpu.roll(full, k, 1)
            out = dot(stencil_out[k * points : (k + 1) * points, :], moved.astype(BF16))
            width = chan_pad - LANES
            first = out[:, :LANES] if carry is None else out[:, :LANES] + carry
            rows_here = slice(m * points, (m + 1) * points)
            spread_out[rows_here, k * width : k * width + LANES] = first.astype(BF16)
            spread_out[rows_here, k * width + LANES : (k + 1) * width] = out[:, LANES:width].astype(BF16)
            carry = out[:, width:]
        spread_out[rows_here, bases * width : bases * width + LANES] = carry.astype(BF16)
    seeded_rows = jnp.concatenate(
        [wide[m, r * slot : r * slot + lon_pad, :chans] for m in range(members) for r in range(rows)], axis=0
    )
    conv = dot(spread_out[:, : bases * chans], w_disco[...], 1, 1)
    hidden = (seeded_rows + conv).astype(BF16)
    hidden_out[...] = hidden
    pre = dot(hidden, w_expand[...])
    rate = math.sqrt(2.0 / math.pi)
    square = pre * pre
    th = jnp.tanh(rate * (pre + 0.044715 * (square * pre)))
    half = 0.5 * (1.0 + th)
    act = (pre * half).astype(BF16)
    gelu_out[...] = act
    slope_out[...] = (half + 0.5 * pre * (1.0 - th * th) * (rate * (1.0 + 3 * 0.044715 * square))).astype(BF16)
    mixed = (hidden.astype(F32) + dot(act, w_reduce[...], 1, 1)).astype(BF16)
    mixed_out[...] = mixed
    turned = dot(w_decode[...], mixed, 1, 1)
    outs = turned.shape[0]
    if up(outs, TILE) > outs:
        turned = jnp.concatenate([turned, jnp.zeros((up(outs, TILE) - outs, turned.shape[1]), F32)], axis=0)
    for q in range(share):
        low, high = q * piece, min((q + 1) * piece, up(outs, TILE))
        if high > low:
            fields_out[q, : high - low, :] = turned[low:high].astype(BF16)
        if high < (q + 1) * piece:
            start = max(high - low, 0)
            fields_out[q, start:, :] = jnp.zeros((piece - start, turned.shape[1]), BF16)


def crps_body(count, points, members, total, *refs):
    fields = [ref[...].astype(F32) for ref in refs[:count]]
    observed = refs[count][...].astype(F32)
    outs = refs[count + 1 :]
    turned = [[f] + [pltpu.roll(f, t * points, 1) for t in range(1, members)] for f in fields]
    for i in range(count):
        paired = jnp.zeros_like(observed)
        for j in range(count):
            for t in range(members):
                if i == j and t == 0:
                    continue
                paired = paired + slope(fields[i] - turned[j][t])
        outs[i][...] = (slope(fields[i] - observed) - paired * (1.0 / (total - 1))).astype(BF16)


def turn(x):
    n, c = x.shape
    wide = jnp.concatenate([x.astype(F32), jnp.zeros((n, up(c, LANES) - c), F32)], axis=1)
    return jnp.swapaxes(wide, 0, 1)[: up(c, TILE)].astype(BF16)


def misc_rows(count, width):
    return -(-count // width), count - count // width * width


def fold_rows(rows, width, first, into):
    n = rows.shape[1]
    count = -(-n // width)
    if count * width > n:
        rows = jnp.concatenate([rows, jnp.zeros((1, count * width - n), rows.dtype)], axis=1)
    at = lax.broadcasted_iota(jnp.int32, into.shape, 0)
    for t in range(count):
        into = jnp.where(at == first + t, rows[:, t * width : (t + 1) * width], into)
    return into, first + count


def fold_ends(left_turned, left, right, width, at, misc):
    count = right.shape[1]
    last = dot(left_turned[width:], right)
    misc, at = fold_rows(last[0:1], width, at, misc)
    rest = count // width * width
    lanes = dot(turn(right[:, rest:])[:TILE], left[:, :width])
    for i in range(count - rest):
        misc, at = fold_rows(lanes[i : i + 1], width, at, misc)
    return misc, at


class Halves:
    def __init__(self, bit, keep, send):
        self.bit, self.keep, self.send = bit, keep, send
        self.half = keep.shape[0]

    def put(self, row, value):
        value = value.astype(BF16)
        for side in (0, 1):
            low, high = max(row, side * self.half), min(row + value.shape[0], (side + 1) * self.half)
            if low >= high:
                continue
            part = value[low - row : high - row]
            at = slice(low - side * self.half, high - side * self.half)

            @pl.when(self.bit == side)
            def _():
                self.keep[at, :] = part

            @pl.when(self.bit != side)
            def _():
                self.send[at, :] = part

    def zero_from(self, row):
        count = 2 * self.half - row
        if count:
            self.put(row, jnp.zeros((count, self.keep.shape[1]), F32))


def backward_body(dims, scale, place, *refs):
    share, piece, outs, chans, hidden_units, width, taps_count = dims
    grads = refs[:share]
    (
        w_decode, w_reduce, w_expand, slopes, hidden, gelu, mixed, spread,
        keep, send, hidden_grad_out, hidden_turned, mixed_turned, turned_grad,
    ) = refs[share:]
    for d in range(share):
        turned_grad[pl.ds(pl.multiple_of(lax.rem(place[0] + d, share) * piece, TILE), piece), :] = grads[d][...]
    field_t = turned_grad[: up(outs, TILE)]
    packed = Halves(place[1], keep, send)
    field = jnp.swapaxes(field_t.astype(F32), 0, 1).astype(BF16)[:, :outs]
    mixed_grad = dot(field, w_decode[...]).astype(BF16)
    gelu_grad = dot(mixed_grad, w_reduce[...])
    pre_grad = (gelu_grad * slopes[...].astype(F32)).astype(BF16)
    hidden_grad = (mixed_grad.astype(F32) + dot(pre_grad, w_expand[...], 1, 1)).astype(BF16)
    hidden_grad_out[...] = hidden_grad
    hidden_grad_t = turn(hidden_grad)
    hidden_turned[...] = hidden_grad_t
    mixed_grad_t = turn(mixed_grad)
    mixed_turned[...] = mixed_grad_t
    hidden_t = turn(hidden[...])
    row = 0
    for part in range(hidden_units // width):
        packed.put(row, dot(hidden_t[:width], pre_grad[:, part * width : (part + 1) * width]) * scale)
        row += width
    decode_grad = dot(field_t[:outs], mixed[:, :width]) * scale
    if up(outs, TILE) > outs:
        decode_grad = jnp.concatenate([decode_grad, jnp.zeros((up(outs, TILE) - outs, width), F32)], axis=0)
    packed.put(row, decode_grad)
    row += up(outs, TILE)
    misc = jnp.zeros((misc_height(chans, hidden_units, outs, taps_count, width), width), F32)
    misc, at = fold_ends(hidden_t, hidden[...], pre_grad, width, 0, misc)
    misc, at = fold_ends(mixed_grad_t, mixed_grad, gelu[...], width, at, misc)
    misc, at = fold_ends(hidden_grad_t, hidden_grad, spread[:, :taps_count], width, at, misc)
    tail = dot(turn(mixed[:, width:])[:TILE], field)
    misc, at = fold_rows(tail[0:1], width, at, misc)
    packed.put(row, misc * scale)
    packed.zero_from(row + misc.shape[0])


def misc_height(chans, hidden_units, outs, taps_count, width):
    return up(2 * sum(misc_rows(hidden_units, width)) + sum(misc_rows(taps_count, width)) + 1, TILE)


def product_body(scale, width, blocks, place, *refs):
    packed = Halves(place[1], refs[-2], refs[-1])
    row = 0
    for left, right, part in blocks:
        packed.put(row, dot(refs[left][:width, :], refs[right][:, part * width : (part + 1) * width]) * scale)
        row += width
    packed.zero_from(row)


def put_matrix(out, block_of, misc, at, width):
    count = out.shape[1]
    for part in range(count // width):
        out[:width, part * width : (part + 1) * width] = block_of(part)
    wide, lanes = misc_rows(count, width)
    rest = count // width * width
    if lanes:
        ends = jnp.swapaxes(misc[at + wide : at + wide + lanes], 0, 1)
        out[:width, rest:] = ends.astype(BF16)
    for t in range(wide):
        size = min(width, count - t * width)
        out[width : width + 1, t * width : t * width + size] = misc[at + t : at + t + 1, :size].astype(BF16)
    return at + wide + lanes


def finish_first_body(dims, summed, expand_out, decode_out, misc_out):
    chans, hidden_units, outs, taps_count, width = dims
    base = hidden_units // width * width
    height = misc_out.shape[0]
    misc_out[...] = summed[base + up(outs, TILE) : base + up(outs, TILE) + height, :]
    misc = misc_out[...].astype(F32)
    put_matrix(expand_out, lambda part: summed[part * width : (part + 1) * width, :], misc, 0, width)
    decode_out[:, :width] = summed[base : base + outs, :]
    at = 2 * sum(misc_rows(hidden_units, width)) + sum(misc_rows(taps_count, width))
    turned = jnp.swapaxes(misc[at : at + 8], 0, 1)
    decode_out[:, width:] = turned[:outs, : decode_out.shape[1] - width].astype(BF16)


def finish_rest_body(dims, second, third, misc_ref, reduce_out, disco_out):
    hidden_units, taps_count, width = dims
    misc = misc_ref[...].astype(F32)
    at = sum(misc_rows(hidden_units, width))
    blocks = hidden_units // width
    at = put_matrix(reduce_out, lambda part: second[part * width : (part + 1) * width, :], misc, at, width)
    put_matrix(
        disco_out,
        lambda part: second[blocks * width : (blocks + 1) * width, :] if part == 0 else third[(part - 1) * width : part * width, :],
        misc, at, width,
    )


def collect_body(dims, hidden_grad, w_disco, stencil, out, left_out, right_out):
    members, rows, lons, chans, lon_pad, slot, bases = dims
    chan_pad = up(chans, LANES)
    points = rows * lon_pad
    width = chan_pad - LANES
    full = bases * width + LANES
    grad = dot(hidden_grad[...], w_disco[...]).astype(BF16)
    grad = jnp.concatenate([grad, jnp.zeros((grad.shape[0], full - grad.shape[1]), BF16)], axis=1)
    for m in range(members):
        total = None
        for k in range(bases):
            part = dot(stencil[k * points : (k + 1) * points, :], grad[m * points : (m + 1) * points, k * width : k * width + chan_pad], 0, 0)
            part = part if k == 0 else pltpu.roll(part, chan_pad - k, 1)
            total = part if total is None else total + part
        for r in range(rows):
            at = r * slot
            own = hidden_grad[m * points + r * lon_pad : m * points + (r + 1) * lon_pad, :].astype(F32)
            out[m, r] = (own + total[at : at + lon_pad, :chans])[:lons]
            left_out[m, r] = total[at + lon_pad : at + lon_pad + 8, :chans][:reach]
            right_out[m, r] = total[at + lon_pad + 8 : at + lon_pad + 16, :chans][:reach]


def bits_of(axis):
    size, out, bit = lax.axis_size(axis), [], 1
    while bit < size:
        out.append((axis, bit))
        bit *= 2
    return out


def swap(x, pair):
    members, lons = lax.axis_size("member"), lax.axis_size("lon")
    perm = []
    for m in range(members):
        for n in range(lons):
            axis, bit = pair[n % 2]
            to = (m ^ bit) * lons + n if axis == "member" else m * lons + (n ^ bit)
            perm.append((m * lons + n, to))
    return lax.ppermute(x, ("member", "lon"), perm)


def my_bit(pair):
    bits = [lax.axis_index(axis) // bit % 2 for axis, bit in pair]
    return jnp.where(lax.axis_index("lon") % 2 == 0, bits[0], bits[1])


def add_rounded(a, b):
    return (a.astype(F32) + b.astype(F32)).astype(BF16)


def streams():
    core, *lon = bits_of("lon")
    mem = bits_of("member")
    orders = [mem[:1] + lon + mem[1:], lon + mem, lon[1:] + mem[:1] + lon[:1] + mem[1:]]
    return [[(d, d) for d in [core] + order] for order in orders]


def row_unit():
    return 8 * 2 ** (len(streams()[0]) - 1)


class Stream:
    def __init__(self, keep, send, order):
        self.kept, self.order = keep, order
        self.got = swap(send, order[0])
        self.bits = [my_bit(order[0])]
        self.steps = [self.halve] * (len(order) - 2) + [self.exchange, self.added] + [self.join] * (len(order) - 1)

    def advance(self, last=None):
        if last is not None and last is not self:
            self.got, last.kept = lax.optimization_barrier((self.got, last.kept))
        self.steps.pop(0)()
        return self

    def halve(self):
        pair = self.order[len(self.bits)]
        count, bit = self.kept.shape[0] // 2, my_bit(pair)
        parts = [
            add_rounded(*(lax.dynamic_slice_in_dim(x, which * count, count, axis=0) for x in (self.kept, self.got)))
            for which in (1 - bit, bit)
        ]
        self.got, self.kept = swap(parts[0], pair), parts[1]
        self.bits.append(bit)

    def exchange(self):
        self.kept = add_rounded(self.kept, self.got)
        self.got = swap(self.kept, self.order[-1])

    def added(self):
        self.kept = add_rounded(self.kept, self.got)
        self.send_back()

    def join(self):
        low = self.bits.pop() == 0
        self.kept = jnp.concatenate([jnp.where(low, self.kept, self.got), jnp.where(low, self.got, self.kept)], axis=0)
        self.send_back()

    def send_back(self):
        if self.bits:
            self.got = swap(self.kept, self.order[len(self.bits) - 1])


def shifted(x, axis, by):
    size = lax.axis_size(axis)
    return lax.ppermute(x, axis, [(i, (i + by) % size) for i in range(size)])


def spread_out(piece_of, axis):
    size = lax.axis_size(axis)
    return [piece_of(0)] + [shifted(piece_of(size - d), axis, -d) for d in range(1, size)]


def per_device(
    latent, member_seeds, member_table, row_bands, disco_basis, w_disco, w_expand, w_reduce, w_decode, target
):
    members, rows, lons, chans = latent.shape
    bases = disco_basis.shape[1]
    hidden_units = w_expand.shape[1]
    outs = w_decode.shape[1]
    share = lax.axis_size("member")
    total_members = members * share
    lon_pad = up(lons, TILE)
    slot = lon_pad + TILE
    points = rows * lon_pad
    flat = members * points
    width = chans // LANES * LANES
    full = bases * width + LANES
    piece = TILE * -(-up(outs, TILE) // (TILE * share))
    me = lax.axis_index("member")
    by_lon = jnp.swapaxes(latent, 1, 2)
    left = jnp.swapaxes(shifted(by_lon[:, lons - reach :], "lon", 1), 1, 2)
    right = jnp.swapaxes(shifted(by_lon[:, :reach], "lon", -1), 1, 2)
    disco_t, reduce_t, decode_t = w_disco.T, w_reduce.T, w_decode.T
    dims = (members, rows, lons, chans, lon_pad, slot, bases, piece, share)
    stencil, spread, hidden, gelu, slopes, mixed, fields = vmem_call(
        functools.partial(forward_body, dims),
        [
            ((bases * points, rows * slot), BF16),
            ((flat, full), BF16),
            ((flat, chans), BF16),
            ((flat, hidden_units), BF16),
            ((flat, hidden_units), BF16),
            ((flat, chans), BF16),
            ((share, piece, flat), BF16),
        ],
        [
            member_seeds, row_bands, disco_basis.astype(F32).reshape(-1),
            latent, left, right, member_table, disco_t, w_expand, reduce_t, decode_t,
        ],
        smem=3,
        scratch=[pltpu.VMEM((members, rows * slot, up(chans, LANES)), F32)],
        name="forward",
    )
    observed = jnp.pad(target, ((0, 0), (0, lon_pad - lons), (0, share * piece - outs))).reshape(points, share * piece).T
    observed = jnp.concatenate([observed] * members, axis=1)
    observed = lax.dynamic_slice_in_dim(observed, me * piece, piece, axis=0)
    here = spread_out(lambda d: lax.dynamic_index_in_dim(fields, (me + d) % share, 0, keepdims=False), "member")
    grads = vmem_call(
        functools.partial(crps_body, share, points, members, total_members),
        [((piece, flat), BF16)] * share,
        here + [observed],
        name="crps",
    )
    back = spread_out(lambda d: grads[d], "member")
    scale = 1.0 / math.sqrt(total_members * rows * lons * lax.axis_size("lon"))
    unit = row_unit()
    taps_count = bases * chans
    height = hidden_units // width * width + up(outs, TILE) + misc_height(chans, hidden_units, outs, taps_count, width)
    place = jnp.stack([me, lax.axis_index("lon") % 2]).astype(jnp.int32)
    orders = streams()

    def halves(rows):
        return [((up(rows, unit) // 2, width), BF16)] * 2

    keep, send, hidden_grad, hidden_turned, mixed_turned = vmem_call(
        functools.partial(backward_body, (share, piece, outs, chans, hidden_units, width, taps_count), scale),
        halves(height) + [
            ((flat, chans), BF16),
            ((up(chans, TILE), flat), BF16),
            ((up(chans, TILE), flat), BF16),
        ],
        [place] + back + [decode_t, reduce_t, w_expand, slopes, hidden, gelu, mixed, spread],
        smem=1,
        scratch=[pltpu.VMEM((share * piece, flat), BF16)],
        name="backward",
    )
    first = Stream(keep, send, orders[0])
    blocks = hidden_units // width
    keep, send = vmem_call(
        functools.partial(product_body, scale, width, [(0, 1, p) for p in range(blocks)] + [(2, 3, 0)]),
        halves((blocks + 1) * width),
        [place, mixed_turned, gelu, hidden_turned, spread],
        smem=1,
        name="second_products",
    )
    second = Stream(keep, send, orders[1])
    first.advance()
    hidden_turned, first.kept = lax.optimization_barrier((hidden_turned, first.kept))
    wide_blocks = taps_count // width
    keep, send = vmem_call(
        functools.partial(product_body, scale, width, [(0, 1, p) for p in range(1, wide_blocks)]),
        halves((wide_blocks - 1) * width),
        [place, hidden_turned, spread],
        smem=1,
        name="third_products",
    )
    third = Stream(keep, send, orders[2])
    second.advance()
    last = third.advance(second)
    hidden_grad, third.kept = lax.optimization_barrier((hidden_grad, third.kept))
    dims = (members, rows, lons, chans, lon_pad, slot, bases)
    latent_grad, to_left, to_right = vmem_call(
        functools.partial(collect_body, dims),
        [(latent.shape, F32), ((members, rows, reach, chans), F32), ((members, rows, reach, chans), F32)],
        [hidden_grad, disco_t, stencil],
        name="collect",
    )
    first.got, latent_grad = lax.optimization_barrier((first.got, latent_grad))
    from_right = shifted(to_left, "lon", -1)
    from_left = shifted(to_right, "lon", 1)
    while third.steps:
        for stream in (first, second, third):
            if stream.steps:
                last = stream.advance(last)
    first, second, third = first.kept, second.kept, third.kept
    grad_expand, decode_grad_t, misc = vmem_call(
        functools.partial(finish_first_body, (chans, hidden_units, outs, taps_count, width)),
        [
            (w_expand.shape, BF16),
            (decode_t.shape, BF16),
            ((misc_height(chans, hidden_units, outs, taps_count, width), width), BF16),
        ],
        [first],
        name="finish_first",
    )
    reduce_grad_t, disco_grad_t = vmem_call(
        functools.partial(finish_rest_body, (hidden_units, taps_count, width)),
        [(reduce_t.shape, BF16), (disco_t.shape, BF16)],
        [second, third, misc],
        name="finish_rest",
    )
    edge = [(0, 0, 0)] * 2
    latent_grad = (
        latent_grad
        + lax.pad(from_right, jnp.float32(0), edge + [(lons - reach, 0, 0), (0, 0, 0)])
        + lax.pad(from_left, jnp.float32(0), edge + [(0, lons - reach, 0), (0, 0, 0)])
    ).astype(BF16)

    return latent_grad, disco_grad_t.T, grad_expand, reduce_grad_t.T, decode_grad_t.T


def solution(mesh):
    placed = (
        P("member", None, "lon", None),
        P("member"),
        P(),
        P(),
        P(),
        P(),
        P(),
        P(),
        P(),
        P(None, "lon", None),
    )
    return jax.shard_map(
        per_device,
        mesh=mesh,
        in_specs=placed,
        out_specs=(P("member", None, "lon", None), P(), P(), P(), P()),
        check_vma=False,
    )
```

```python
import functools
import math

import jax
import jax.numpy as jnp
from jax import lax
from jax.experimental import pallas as pl
from jax.experimental.pallas import tpu as pltpu
from jax.sharding import PartitionSpec as P

reach = 3
taps = 2 * reach + 1
smooth = 0.5
LANES = 128
TILE = 16
VMEM_LIMIT = 24 * 2**20
BEGIN = 48
F32 = jnp.float32
BF16 = jnp.bfloat16


def up(value, unit):
    return -(-value // unit) * unit


def dot(a, b, ca=1, cb=0):
    return lax.dot_general(a, b, (((ca,), (cb,)), ((), ())), preferred_element_type=F32)


def slope(d):
    return d * lax.rsqrt(d * d + smooth * smooth)


def vmem_call(body, outs, args, smem=0, scratch=(), name=None, moved=0):
    specs = [pl.BlockSpec(memory_space=pltpu.SMEM)] * smem
    specs += [pl.BlockSpec(memory_space=pltpu.VMEM)] * (len(args) - smem)
    return pl.pallas_call(
        body,
        out_shape=[jax.ShapeDtypeStruct(shape, dtype) for shape, dtype in outs],
        in_specs=specs,
        out_specs=[pl.BlockSpec(memory_space=pltpu.VMEM)] * len(outs),
        scratch_shapes=list(scratch),
        compiler_params=pltpu.CompilerParams(vmem_limit_bytes=VMEM_LIMIT),
        cost_estimate=pl.CostEstimate(flops=0, bytes_accessed=moved, transcendentals=0),
        name=name,
    )(*args)


def begin_body(x, out):
    out[...] = x[...]


def prepare_body(dims, seeds, bands, basis, table, stencil_out, offsets_out):
    members, rows, lons, chans, lon_pad, slot, bases, piece, share = dims
    points = rows * lon_pad
    per_tile = LANES // slot
    lane = lax.broadcasted_iota(jnp.int32, (lon_pad, LANES), 1)
    lon = lax.broadcasted_iota(jnp.int32, (lon_pad, LANES), 0)
    place = lane % slot
    own = place < lons
    before = (place >= lon_pad) & (place < lon_pad + reach)
    after = (place >= lon_pad + 8) & (place < lon_pad + 8 + reach)
    wide_lon = jnp.where(own, place + reach, jnp.where(before, place - lon_pad, place - lon_pad - 8 + lons + reach))
    tap = jnp.where((own | before | after) & (lon < lons), wide_lon - lon, -1)
    tap = jnp.where(lane < slot, tap, tap + 1000 * (lane // slot))
    masks = [[tap == 1000 * part + b for b in range(taps)] for part in range(per_tile)]
    for r in range(rows):
        band = bands[r]
        for k in range(bases):
            for t in range(rows // per_tile):
                block = jnp.zeros((lon_pad, LANES), F32)
                for part in range(per_tile):
                    a = t * per_tile + part - r + reach
                    if not 0 <= a < taps:
                        continue
                    base = ((band * bases + k) * taps + a) * taps
                    for b in range(taps):
                        block = jnp.where(masks[part][b], basis[base + b], block)
                stencil_out[k * points + r * lon_pad : k * points + (r + 1) * lon_pad, t * LANES : (t + 1) * LANES] = block.astype(BF16)
    seed_count = table.shape[0]
    mrow = lax.broadcasted_iota(jnp.int32, (TILE, seed_count), 0)
    mcol = lax.broadcasted_iota(jnp.int32, (TILE, seed_count), 1)
    onehot = jnp.zeros((TILE, seed_count), F32)
    for m in range(members):
        onehot = jnp.where((mrow == m) & (mcol == seeds[m]), 1.0, onehot)
    offsets_out[...] = dot(onehot.astype(BF16), table[...])


def forward_body(
    dims, place, latent, left, right, stencil, offsets_in, w_disco, w_expand, w_reduce, w_decode, *refs
):
    members, rows, lons, chans, lon_pad, slot, bases, piece, share = dims
    spread_out, hidden_out, gelu_out, slope_out, mixed_out = refs[:5]
    fields_out = refs[5 : 5 + share]
    wide, turned_fields = refs[5 + share :]
    chan_pad = up(chans, LANES)
    points = rows * lon_pad
    offsets = offsets_in[...]
    wide[...] = jnp.zeros_like(wide)
    for m in range(members):
        off = offsets[m : m + 1, :]
        for r in range(rows):
            for ref, start, count in ((latent, 0, lons), (left, lon_pad, reach), (right, lon_pad + 8, reach)):
                seeded = (ref[m, r].astype(F32) + off).astype(BF16).astype(F32)
                wide[m, r * slot + start : r * slot + start + count, :chans] = seeded
    for m in range(members):
        full = wide[m]
        carry = None
        for k in range(bases):
            moved = full if k == 0 else pltpu.roll(full, k, 1)
            out = dot(stencil[k * points : (k + 1) * points, :], moved.astype(BF16))
            width = chan_pad - LANES
            first = out[:, :LANES] if carry is None else out[:, :LANES] + carry
            rows_here = slice(m * points, (m + 1) * points)
            spread_out[rows_here, k * width : k * width + LANES] = first.astype(BF16)
            spread_out[rows_here, k * width + LANES : (k + 1) * width] = out[:, LANES:width].astype(BF16)
            carry = out[:, width:]
        spread_out[rows_here, bases * width : bases * width + LANES] = carry.astype(BF16)
    seeded_rows = jnp.concatenate(
        [wide[m, r * slot : r * slot + lon_pad, :chans] for m in range(members) for r in range(rows)], axis=0
    )
    conv = dot(spread_out[:, : bases * chans], w_disco[...], 1, 1)
    hidden = (seeded_rows + conv).astype(BF16)
    hidden_out[...] = hidden
    pre = dot(hidden, w_expand[...])
    rate = math.sqrt(2.0 / math.pi)
    square = pre * pre
    th = jnp.tanh(rate * (pre + 0.044715 * (square * pre)))
    half = 0.5 * (1.0 + th)
    act = (pre * half).astype(BF16)
    gelu_out[...] = act
    slope_out[...] = (half + 0.5 * pre * (1.0 - th * th) * (rate * (1.0 + 3 * 0.044715 * square))).astype(BF16)
    mixed = (hidden.astype(F32) + dot(act, w_reduce[...], 1, 1)).astype(BF16)
    mixed_out[...] = mixed
    turned = dot(w_decode[...], mixed, 1, 1).astype(BF16)
    outs = turned.shape[0]
    if share * piece > outs:
        turned = jnp.concatenate([turned, jnp.zeros((share * piece - outs, turned.shape[1]), BF16)], axis=0)
    turned_fields[...] = turned
    for d in range(share):
        fields_out[d][...] = turned_fields[pl.ds(pl.multiple_of(lax.rem(place[0] + d, share) * piece, TILE), piece), :]


def crps_body(count, points, members, total, *refs):
    fields = [ref[...].astype(F32) for ref in refs[:count]]
    observed = refs[count][...].astype(F32)
    outs = refs[count + 1 :]
    turned = [[f] + [pltpu.roll(f, t * points, 1) for t in range(1, members)] for f in fields]
    for i in range(count):
        paired = jnp.zeros_like(observed)
        for j in range(count):
            for t in range(members):
                if i == j and t == 0:
                    continue
                paired = paired + slope(fields[i] - turned[j][t])
        outs[i][...] = (slope(fields[i] - observed) - paired * (1.0 / (total - 1))).astype(BF16)


def turn(x):
    n, c = x.shape
    wide = jnp.concatenate([x.astype(F32), jnp.zeros((n, up(c, LANES) - c), F32)], axis=1)
    return jnp.swapaxes(wide, 0, 1)[: up(c, TILE)].astype(BF16)


def misc_rows(count, width):
    return -(-count // width), count - count // width * width


def fold_rows(rows, width, first, into):
    n = rows.shape[1]
    count = -(-n // width)
    if count * width > n:
        rows = jnp.concatenate([rows, jnp.zeros((1, count * width - n), rows.dtype)], axis=1)
    at = lax.broadcasted_iota(jnp.int32, into.shape, 0)
    for t in range(count):
        into = jnp.where(at == first + t, rows[:, t * width : (t + 1) * width], into)
    return into, first + count


def fold_ends(left_turned, left, right, width, at, misc):
    count = right.shape[1]
    last = dot(left_turned[width:], right)
    misc, at = fold_rows(last[0:1], width, at, misc)
    rest = count // width * width
    lanes = dot(turn(right[:, rest:])[:TILE], left[:, :width])
    for i in range(count - rest):
        misc, at = fold_rows(lanes[i : i + 1], width, at, misc)
    return misc, at


class Halves:
    def __init__(self, bit, keep, send):
        self.bit, self.keep, self.send = bit, keep, send
        self.half = keep.shape[0]

    def put(self, row, value):
        value = value.astype(BF16)
        for side in (0, 1):
            low, high = max(row, side * self.half), min(row + value.shape[0], (side + 1) * self.half)
            if low >= high:
                continue
            part = value[low - row : high - row]
            at = slice(low - side * self.half, high - side * self.half)

            @pl.when(self.bit == side)
            def _():
                self.keep[at, :] = part

            @pl.when(self.bit != side)
            def _():
                self.send[at, :] = part

    def zero_from(self, row):
        count = 2 * self.half - row
        if count:
            self.put(row, jnp.zeros((count, self.keep.shape[1]), F32))


def first_body(dims, scale, place, *refs):
    share, piece, outs, hidden_units, width = dims
    grads = refs[:share]
    w_decode, gelu, mixed, keep, send, mixed_grad_out, mixed_turned, field_out, turned_grad = refs[share:]
    for d in range(share):
        turned_grad[pl.ds(pl.multiple_of(lax.rem(place[0] + d, share) * piece, TILE), piece), :] = grads[d][...]
    field_t = turned_grad[: up(outs, TILE)]
    field_out[...] = field_t
    packed = Halves(place[1], keep, send)
    field = jnp.swapaxes(field_t.astype(F32), 0, 1).astype(BF16)[:, :outs]
    mixed_grad = dot(field, w_decode[...]).astype(BF16)
    mixed_grad_out[...] = mixed_grad
    mixed_grad_t = turn(mixed_grad)
    mixed_turned[...] = mixed_grad_t
    row = 0
    for part in range(hidden_units // width):
        packed.put(row, dot(mixed_grad_t[:width], gelu[:, part * width : (part + 1) * width]) * scale)
        row += width
    decode_grad = dot(field_t[:outs], mixed[:, :width]) * scale
    if up(outs, TILE) > outs:
        decode_grad = jnp.concatenate([decode_grad, jnp.zeros((up(outs, TILE) - outs, width), F32)], axis=0)
    packed.put(row, decode_grad)
    packed.zero_from(row + up(outs, TILE))


def second_body(dims, scale, place, *refs):
    outs, chans, hidden_units, width, taps_count = dims
    (
        mixed_grad_in, mixed_turned, field_t, w_reduce, w_expand, slopes, hidden, gelu, mixed, spread,
        keep, send, hidden_grad_out, hidden_turned,
    ) = refs
    packed = Halves(place[1], keep, send)
    mixed_grad = mixed_grad_in[...]
    gelu_grad = dot(mixed_grad, w_reduce[...])
    pre_grad = (gelu_grad * slopes[...].astype(F32)).astype(BF16)
    hidden_grad = (mixed_grad.astype(F32) + dot(pre_grad, w_expand[...], 1, 1)).astype(BF16)
    hidden_grad_out[...] = hidden_grad
    hidden_grad_t = turn(hidden_grad)
    hidden_turned[...] = hidden_grad_t
    hidden_t = turn(hidden[...])
    row = 0
    for part in range(hidden_units // width):
        packed.put(row, dot(hidden_t[:width], pre_grad[:, part * width : (part + 1) * width]) * scale)
        row += width
    packed.put(row, dot(hidden_grad_t[:width], spread[:, :width]) * scale)
    row += width
    misc = jnp.zeros((misc_height(chans, hidden_units, outs, taps_count, width), width), F32)
    misc, at = fold_ends(hidden_t, hidden[...], pre_grad, width, 0, misc)
    misc, at = fold_ends(mixed_turned[...], mixed_grad, gelu[...], width, at, misc)
    misc, at = fold_ends(hidden_grad_t, hidden_grad, spread[:, :taps_count], width, at, misc)
    tail = dot(turn(mixed[:, width:])[:TILE], field_t[:outs], 1, 1)
    misc, at = fold_rows(tail[0:1], width, at, misc)
    packed.put(row, misc * scale)
    packed.zero_from(row + misc.shape[0])


def misc_height(chans, hidden_units, outs, taps_count, width):
    return up(2 * sum(misc_rows(hidden_units, width)) + sum(misc_rows(taps_count, width)) + 1, TILE)


def third_body(scale, width, place, left, right, keep, send):
    packed = Halves(place[1], keep, send)
    row = 0
    while row < keep.shape[0] * 2 // width * width:
        at = row + width
        packed.put(row, dot(left[:width, :], right[:, at : at + width]) * scale)
        row += width
    packed.zero_from(row)


def combine_body(index, place, kept, got, send, keep):
    count = keep.shape[0]
    for target, side in ((send, 1 - place[index]), (keep, place[index])):
        rows = pl.ds(pl.multiple_of(side * count, TILE), count)
        target[...] = add_rounded(kept[rows, :], got[rows, :])


class Joined:
    def __init__(self, bit, kept, got):
        self.bit, self.halves = bit, (kept, got)
        self.half = kept.shape[0]

    def parts(self, row, count):
        for side in (0, 1):
            low, high = max(row, side * self.half), min(row + count, (side + 1) * self.half)
            if low < high:
                kept, got = (ref[low - side * self.half : high - side * self.half, :] for ref in self.halves)
                yield low - row, jnp.where(self.bit == side, kept, got)


def put_matrix(out, block_of, misc, at, width):
    count = out.shape[1]
    for part in range(count // width):
        source, row = block_of(part)
        for offset, value in source.parts(row, width):
            out[offset : offset + value.shape[0], part * width : (part + 1) * width] = value
    wide, lanes = misc_rows(count, width)
    rest = count // width * width
    if lanes:
        ends = jnp.swapaxes(misc[at + wide : at + wide + lanes], 0, 1)
        out[:width, rest:] = ends.astype(BF16)
    for t in range(wide):
        size = min(width, count - t * width)
        out[width : width + 1, t * width : t * width + size] = misc[at + t : at + t + 1, :size].astype(BF16)
    return at + wide + lanes


def finish_second_body(dims, place, kept, got, expand_out, misc_out):
    hidden_units, width = dims
    source = Joined(place[1], kept, got)
    for offset, value in source.parts((hidden_units // width + 1) * width, misc_out.shape[0]):
        misc_out[offset : offset + value.shape[0], :] = value
    put_matrix(expand_out, lambda part: (source, part * width), misc_out[...].astype(F32), 0, width)


def finish_first_body(dims, place, kept, got, misc_ref, reduce_out, decode_out):
    hidden_units, outs, taps_count, width = dims
    source = Joined(place[1], kept, got)
    misc = misc_ref[...].astype(F32)
    at = sum(misc_rows(hidden_units, width))
    at = put_matrix(reduce_out, lambda part: (source, part * width), misc, at, width)
    at += sum(misc_rows(taps_count, width))
    for offset, value in source.parts(hidden_units // width * width, outs):
        decode_out[offset : offset + value.shape[0], :width] = value
    turned = jnp.swapaxes(misc[at : at + 8], 0, 1)
    decode_out[:, width:] = turned[:outs, : decode_out.shape[1] - width].astype(BF16)


def finish_third_body(dims, place, kept_second, got_second, kept, got, misc_ref, disco_out):
    hidden_units, width = dims
    second, third = Joined(place[1], kept_second, got_second), Joined(place[1], kept, got)
    first = hidden_units // width * width
    put_matrix(
        disco_out,
        lambda part: (third, (part - 1) * width) if part else (second, first),
        misc_ref[...].astype(F32), 2 * sum(misc_rows(hidden_units, width)), width,
    )


def collect_body(dims, hidden_grad, w_disco, stencil, out, left_out, right_out):
    members, rows, lons, chans, lon_pad, slot, bases = dims
    chan_pad = up(chans, LANES)
    points = rows * lon_pad
    width = chan_pad - LANES
    full = bases * width + LANES
    grad = dot(hidden_grad[...], w_disco[...]).astype(BF16)
    grad = jnp.concatenate([grad, jnp.zeros((grad.shape[0], full - grad.shape[1]), BF16)], axis=1)
    for m in range(members):
        total = None
        for k in range(bases):
            part = dot(stencil[k * points : (k + 1) * points, :], grad[m * points : (m + 1) * points, k * width : k * width + chan_pad], 0, 0)
            part = part if k == 0 else pltpu.roll(part, chan_pad - k, 1)
            total = part if total is None else total + part
        for r in range(rows):
            at = r * slot
            own = hidden_grad[m * points + r * lon_pad : m * points + (r + 1) * lon_pad, :].astype(F32)
            out[m, r] = (own + total[at : at + lon_pad, :chans])[:lons]
            left_out[m, r] = total[at + lon_pad : at + lon_pad + 8, :chans][:reach]
            right_out[m, r] = total[at + lon_pad + 8 : at + lon_pad + 16, :chans][:reach]


def bits_of(axis):
    size, out, bit = lax.axis_size(axis), [], 1
    while bit < size:
        out.append((axis, bit))
        bit *= 2
    return out


def swap(x, pair):
    members, lons = lax.axis_size("member"), lax.axis_size("lon")
    perm = []
    for m in range(members):
        for n in range(lons):
            axis, bit = pair[n % 2]
            to = (m ^ bit) * lons + n if axis == "member" else m * lons + (n ^ bit)
            perm.append((m * lons + n, to))
    return lax.ppermute(x, ("member", "lon"), perm)


def add_rounded(a, b):
    return (a.astype(F32) + b.astype(F32)).astype(BF16)


def streams():
    core, *lon = bits_of("lon")
    mem = bits_of("member")
    orders = [mem[:1] + lon + mem[1:], lon + mem, lon[1:] + mem[:1] + lon[:1] + mem[1:]]
    return [[core] + order for order in orders]


def row_unit():
    return 8 * 2 ** (len(streams()[0]) - 1)


def all_dims():
    return bits_of("lon") + bits_of("member")


class Stream:
    def __init__(self, place, keep, send, order):
        self.place, self.kept, self.order = place, keep, order
        self.got = swap(send, (order[0], order[0]))
        self.done = [order[0]]
        self.steps = [self.halve] * (len(order) - 2) + [self.exchange, self.added] + [self.join] * (len(order) - 2)

    def advance(self, last=None):
        if last is not None and last is not self:
            self.got, last.kept = lax.optimization_barrier((self.got, last.kept))
        self.steps.pop(0)()
        return self

    def halve(self):
        dim = self.order[len(self.done)]
        count, index = self.kept.shape[0] // 2, 1 + all_dims().index(dim)
        if count % TILE == 0 and len(self.done) < 3:
            shape = ((count, self.kept.shape[1]), BF16)
            args = [self.place, self.kept, self.got]
            send, keep = vmem_call(functools.partial(combine_body, index), [shape] * 2, args, smem=1, name="combine")
        else:
            bit = self.place[index]
            send, keep = (
                add_rounded(*(lax.dynamic_slice_in_dim(x, side * count, count, axis=0) for x in (self.kept, self.got)))
                for side in (1 - bit, bit)
            )
        self.got, self.kept = swap(send, (dim, dim)), keep
        self.done.append(dim)

    def exchange(self):
        self.kept = add_rounded(self.kept, self.got)
        self.got = swap(self.kept, (self.order[-1],) * 2)

    def added(self):
        self.kept = add_rounded(self.kept, self.got)
        self.send_back()

    def join(self):
        low = self.place[1 + all_dims().index(self.done.pop())] == 0
        self.kept = jnp.concatenate([jnp.where(low, self.kept, self.got), jnp.where(low, self.got, self.kept)], axis=0)
        self.send_back()

    def send_back(self):
        self.got = swap(self.kept, (self.done[-1],) * 2)


def shifted(x, axis, by):
    size = lax.axis_size(axis)
    return lax.ppermute(x, axis, [(i, (i + by) % size) for i in range(size)])


def spread_out(piece_of, axis):
    size = lax.axis_size(axis)
    return [piece_of(0)] + [shifted(piece_of(size - d), axis, -d) for d in range(1, size)]


def per_device(
    latent, member_seeds, member_table, row_bands, disco_basis, w_disco, w_expand, w_reduce, w_decode, target
):
    members, rows, lons, chans = latent.shape
    bases = disco_basis.shape[1]
    hidden_units = w_expand.shape[1]
    outs = w_decode.shape[1]
    share = lax.axis_size("member")
    total_members = members * share
    lon_pad = up(lons, TILE)
    slot = lon_pad + TILE
    points = rows * lon_pad
    flat = members * points
    width = chans // LANES * LANES
    full = bases * width + LANES
    piece = TILE * -(-up(outs, TILE) // (TILE * share))
    me = lax.axis_index("member")
    place = jnp.stack([me] + [lax.axis_index(axis) // bit % 2 for axis, bit in all_dims()]).astype(jnp.int32)
    (row_bands,) = vmem_call(
        begin_body, [(row_bands.shape, row_bands.dtype)], [row_bands], name="begin", moved=BEGIN * 2**20
    )
    row_bands, latent = lax.optimization_barrier((row_bands, latent))
    by_lon = jnp.swapaxes(latent, 1, 2)
    left = jnp.swapaxes(shifted(by_lon[:, lons - reach :], "lon", 1), 1, 2)
    right = jnp.swapaxes(shifted(by_lon[:, :reach], "lon", -1), 1, 2)
    disco_t, reduce_t, decode_t = w_disco.T, w_reduce.T, w_decode.T
    dims = (members, rows, lons, chans, lon_pad, slot, bases, piece, share)
    stencil, offsets = vmem_call(
        functools.partial(prepare_body, dims),
        [((bases * points, rows * slot), BF16), ((TILE, chans), F32)],
        [member_seeds, row_bands, disco_basis.astype(F32).reshape(-1), member_table],
        smem=3,
        name="prepare",
        moved=4 * 2**20,
    )
    weights = [disco_t, w_expand, reduce_t, decode_t]
    spread, hidden, gelu, slopes, mixed, *here = vmem_call(
        functools.partial(forward_body, dims),
        [
            ((flat, full), BF16),
            ((flat, chans), BF16),
            ((flat, hidden_units), BF16),
            ((flat, hidden_units), BF16),
            ((flat, chans), BF16),
        ]
        + [((piece, flat), BF16)] * share,
        [place, latent, left, right, stencil, offsets] + weights,
        smem=1,
        scratch=[
            pltpu.VMEM((members, rows * slot, up(chans, LANES)), F32),
            pltpu.VMEM((share * piece, flat), BF16),
        ],
        name="forward",
        moved=24 * 2**20,
    )
    here_out = here
    observed = jnp.pad(target, ((0, 0), (0, lon_pad - lons), (0, share * piece - outs))).reshape(points, share * piece).T
    observed = jnp.concatenate([observed] * members, axis=1)
    observed = lax.dynamic_slice_in_dim(observed, me * piece, piece, axis=0)
    here = spread_out(lambda d: here_out[d], "member")
    grads = vmem_call(
        functools.partial(crps_body, share, points, members, total_members),
        [((piece, flat), BF16)] * share,
        here + [observed],
        name="crps",
        moved=3 * 2**20,
    )
    back = spread_out(lambda d: grads[d], "member")
    scale = 1.0 / math.sqrt(total_members * rows * lons * lax.axis_size("lon"))
    unit = row_unit()
    taps_count = bases * chans
    orders = streams()

    def halves(rows):
        return [((up(rows, unit) // 2, width), BF16)] * 2

    turned_shape = ((up(chans, TILE), flat), BF16)
    blocks = hidden_units // width
    keep, send, mixed_grad, mixed_turned, field_turned = vmem_call(
        functools.partial(first_body, (share, piece, outs, hidden_units, width), scale),
        halves(blocks * width + up(outs, TILE)) + [((flat, chans), BF16), turned_shape, ((up(outs, TILE), flat), BF16)],
        [place] + back + [decode_t, gelu, mixed],
        smem=1,
        scratch=[pltpu.VMEM((share * piece, flat), BF16)],
        name="first_products",
        moved=9 * 2**20,
    )
    first = Stream(place, keep, send, orders[0])
    misc_shape = ((misc_height(chans, hidden_units, outs, taps_count, width), width), BF16)
    keep, send, hidden_grad, hidden_turned = vmem_call(
        functools.partial(second_body, (outs, chans, hidden_units, width, taps_count), scale),
        halves((blocks + 1) * width + misc_shape[0][0]) + [((flat, chans), BF16), turned_shape],
        [place, mixed_grad, mixed_turned, field_turned, reduce_t, w_expand, slopes, hidden, gelu, mixed, spread],
        smem=1,
        name="second_products",
    )
    second = Stream(place, keep, send, orders[1])
    first.advance()
    hidden_turned, first.kept = lax.optimization_barrier((hidden_turned, first.kept))
    keep, send = vmem_call(
        functools.partial(third_body, scale, width),
        halves((taps_count // width - 1) * width),
        [place, hidden_turned, spread],
        smem=1,
        name="third_products",
    )
    third = Stream(place, keep, send, orders[2])
    second.advance()
    last = third.advance(second)
    hidden_grad, third.kept = lax.optimization_barrier((hidden_grad, third.kept))
    dims = (members, rows, lons, chans, lon_pad, slot, bases)
    latent_grad, to_left, to_right = vmem_call(
        functools.partial(collect_body, dims),
        [(latent.shape, F32), ((members, rows, reach, chans), F32), ((members, rows, reach, chans), F32)],
        [hidden_grad, disco_t, stencil],
        name="collect",
    )
    first.got, latent_grad = lax.optimization_barrier((first.got, latent_grad))
    from_right = shifted(to_left, "lon", -1)
    from_left = shifted(to_right, "lon", 1)
    for stream in (first, second, third) * 4:
        last = stream.advance(last)
    first.got, from_right, from_left = lax.optimization_barrier((first.got, from_right, from_left))
    edge = [(0, 0, 0)] * 2
    latent_grad = (
        latent_grad
        + lax.pad(from_right, jnp.float32(0), edge + [(lons - reach, 0, 0), (0, 0, 0)])
        + lax.pad(from_left, jnp.float32(0), edge + [(0, lons - reach, 0), (0, 0, 0)])
    ).astype(BF16)

    latent_grad = jnp.swapaxes(latent_grad, 1, 2)
    for stream in (first, second, third):
        last = stream.advance(last)
    first.got, latent_grad = lax.optimization_barrier((first.got, latent_grad))
    while third.steps:
        for stream in (first, second, third):
            if stream.steps:
                last = stream.advance(last)
    grad_expand, misc = vmem_call(
        functools.partial(finish_second_body, (hidden_units, width)),
        [(w_expand.shape, BF16), misc_shape],
        [place, second.kept, second.got],
        smem=1,
        name="finish_second",
    )
    reduce_grad_t, decode_grad_t = vmem_call(
        functools.partial(finish_first_body, (hidden_units, outs, taps_count, width)),
        [(reduce_t.shape, BF16), (decode_t.shape, BF16)],
        [place, first.kept, first.got, misc],
        smem=1,
        name="finish_first",
    )
    (disco_grad_t,) = vmem_call(
        functools.partial(finish_third_body, (hidden_units, width)),
        [(disco_t.shape, BF16)],
        [place, second.kept, second.got, third.kept, third.got, misc],
        smem=1,
        name="finish_third",
    )
    return jnp.swapaxes(latent_grad, 1, 2), disco_grad_t.T, grad_expand, reduce_grad_t.T, decode_grad_t.T


def solution(mesh):
    placed = (
        P("member", None, "lon", None),
        P("member"),
        P(),
        P(),
        P(),
        P(),
        P(),
        P(),
        P(),
        P(None, "lon", None),
    )
    return jax.shard_map(
        per_device,
        mesh=mesh,
        in_specs=placed,
        out_specs=(P("member", None, "lon", None), P(), P(), P(), P()),
        check_vma=False,
    )
```

```python
import functools
import math

import jax
import jax.numpy as jnp
from jax import lax
from jax.experimental import pallas as pl
from jax.experimental.layout import Layout, with_layout_constraint
from jax.experimental.pallas import tpu as pltpu
from jax.sharding import PartitionSpec as P

reach = 3
taps = 2 * reach + 1
smooth = 0.5
LANES = 128
TILE = 16
VMEM_LIMIT = 24 * 2**20
F32 = jnp.float32
BF16 = jnp.bfloat16


def up(value, unit):
    return -(-value // unit) * unit


def dot(a, b, ca=1, cb=0):
    return lax.dot_general(a, b, (((ca,), (cb,)), ((), ())), preferred_element_type=F32)


def slope(d):
    return d * lax.rsqrt(d * d + smooth * smooth)


def vmem_call(body, outs, args, smem=0, scratch=(), name=None, moved=0):
    specs = [pl.BlockSpec(memory_space=pltpu.SMEM)] * smem
    specs += [pl.BlockSpec(memory_space=pltpu.VMEM)] * (len(args) - smem)
    return pl.pallas_call(
        body,
        out_shape=[jax.ShapeDtypeStruct(shape, dtype) for shape, dtype in outs],
        in_specs=specs,
        out_specs=[pl.BlockSpec(memory_space=pltpu.VMEM)] * len(outs),
        scratch_shapes=list(scratch),
        compiler_params=pltpu.CompilerParams(vmem_limit_bytes=VMEM_LIMIT),
        cost_estimate=pl.CostEstimate(flops=0, bytes_accessed=moved, transcendentals=0),
        name=name,
    )(*args)


def prepare_body(dims, seeds, bands, basis, table, stencil_out, offsets_out):
    members, rows, lons, chans, lon_pad, slot, bases, piece, share = dims
    points = rows * lon_pad
    per_tile = LANES // slot
    lane = lax.broadcasted_iota(jnp.int32, (lon_pad, LANES), 1)
    lon = lax.broadcasted_iota(jnp.int32, (lon_pad, LANES), 0)
    place = lane % slot
    own = place < lons
    before = (place >= lon_pad) & (place < lon_pad + reach)
    after = (place >= lon_pad + 8) & (place < lon_pad + 8 + reach)
    wide_lon = jnp.where(own, place + reach, jnp.where(before, place - lon_pad, place - lon_pad - 8 + lons + reach))
    tap = jnp.where((own | before | after) & (lon < lons), wide_lon - lon, -1)
    tap = jnp.where(lane < slot, tap, tap + 1000 * (lane // slot))
    masks = [[tap == 1000 * part + b for b in range(taps)] for part in range(per_tile)]
    for r in range(rows):
        band = bands[r]
        for k in range(bases):
            for t in range(rows // per_tile):
                block = jnp.zeros((lon_pad, LANES), F32)
                for part in range(per_tile):
                    a = t * per_tile + part - r + reach
                    if not 0 <= a < taps:
                        continue
                    base = ((band * bases + k) * taps + a) * taps
                    for b in range(taps):
                        block = jnp.where(masks[part][b], basis[base + b], block)
                stencil_out[k * points + r * lon_pad : k * points + (r + 1) * lon_pad, t * LANES : (t + 1) * LANES] = block.astype(BF16)
    seed_count = table.shape[0]
    mrow = lax.broadcasted_iota(jnp.int32, (TILE, seed_count), 0)
    mcol = lax.broadcasted_iota(jnp.int32, (TILE, seed_count), 1)
    onehot = jnp.zeros((TILE, seed_count), F32)
    for m in range(members):
        onehot = jnp.where((mrow == m) & (mcol == seeds[m]), 1.0, onehot)
    offsets_out[...] = dot(onehot.astype(BF16), table[...])


def forward_body(
    dims, place, latent, left, right, stencil, offsets_in, w_disco, w_expand, *refs
):
    members, rows, lons, chans, lon_pad, slot, bases, piece, share = dims
    spread_out, hidden_out, gelu_out, pre_out, wide = refs
    chan_pad = up(chans, LANES)
    points = rows * lon_pad
    offsets = offsets_in[...]
    wide[...] = jnp.zeros_like(wide)
    for m in range(members):
        off = offsets[m : m + 1, :]
        for r in range(rows):
            for ref, start, count in ((latent, 0, lons), (left, lon_pad, reach), (right, lon_pad + 8, reach)):
                seeded = (ref[m, r].astype(F32) + off).astype(BF16).astype(F32)
                wide[m, r * slot + start : r * slot + start + count, :chans] = seeded
    for m in range(members):
        full = wide[m]
        carry = None
        for k in range(bases):
            moved = full if k == 0 else pltpu.roll(full, k, 1)
            out = dot(stencil[k * points : (k + 1) * points, :], moved.astype(BF16))
            width = chan_pad - LANES
            first = out[:, :LANES] if carry is None else out[:, :LANES] + carry
            rows_here = slice(m * points, (m + 1) * points)
            spread_out[rows_here, k * width : k * width + LANES] = first.astype(BF16)
            spread_out[rows_here, k * width + LANES : (k + 1) * width] = out[:, LANES:width].astype(BF16)
            carry = out[:, width:]
        spread_out[rows_here, bases * width : bases * width + LANES] = carry.astype(BF16)
    seeded_rows = jnp.concatenate(
        [wide[m, r * slot : r * slot + lon_pad, :chans] for m in range(members) for r in range(rows)], axis=0
    )
    conv = dot(spread_out[:, : bases * chans], w_disco[...], 1, 1)
    hidden = (seeded_rows + conv).astype(BF16)
    hidden_out[...] = hidden
    pre = dot(hidden, w_expand[...])
    rate = math.sqrt(2.0 / math.pi)
    square = pre * pre
    th = jnp.tanh(rate * (pre + 0.044715 * (square * pre)))
    half = 0.5 * (1.0 + th)
    act = (pre * half).astype(BF16)
    gelu_out[...] = act
    pre_out[...] = pre


def fields_body(dims, place, hidden_in, act, w_reduce, w_decode, *refs):
    members, rows, lons, chans, lon_pad, slot, bases, piece, share = dims
    mixed_out, fields_out, turned_fields = refs[0], refs[1 : 1 + share], refs[1 + share]
    hidden = hidden_in[...]
    mixed = (hidden.astype(F32) + dot(act[...], w_reduce[...], 1, 1)).astype(BF16)
    mixed_out[...] = mixed
    turned = dot(w_decode[...], mixed, 1, 1).astype(BF16)
    outs = turned.shape[0]
    if share * piece > outs:
        turned = jnp.concatenate([turned, jnp.zeros((share * piece - outs, turned.shape[1]), BF16)], axis=0)
    turned_fields[...] = turned
    for d in range(share):
        fields_out[d][...] = turned_fields[pl.ds(pl.multiple_of((place[0] ^ d) * piece, TILE), piece), :]


def slopes_body(pre_in, hidden, slope_out, hidden_turned):
    rate = math.sqrt(2.0 / math.pi)
    pre = pre_in[...]
    square = pre * pre
    th = jnp.tanh(rate * (pre + 0.044715 * (square * pre)))
    half = 0.5 * (1.0 + th)
    slope_out[...] = (half + 0.5 * pre * (1.0 - th * th) * (rate * (1.0 + 3 * 0.044715 * square))).astype(BF16)
    hidden_turned[...] = turn(hidden[...])


def crps_body(count, points, members, total, *refs):
    fields = [ref[...].astype(F32) for ref in refs[:count]]
    observed = refs[count][...].astype(F32)
    outs = refs[count + 1 :]
    turned = [[f] + [pltpu.roll(f, t * points, 1) for t in range(1, members)] for f in fields]
    for i in range(count):
        paired = jnp.zeros_like(observed)
        for j in range(count):
            for t in range(members):
                if i == j and t == 0:
                    continue
                paired = paired + slope(fields[i] - turned[j][t])
        outs[i][...] = (slope(fields[i] - observed) - paired * (1.0 / (total - 1))).astype(BF16)


def turn(x):
    n, c = x.shape
    wide = jnp.concatenate([x.astype(F32), jnp.zeros((n, up(c, LANES) - c), F32)], axis=1)
    return jnp.swapaxes(wide, 0, 1)[: up(c, TILE)].astype(BF16)


def misc_rows(count, width):
    return -(-count // width), count - count // width * width


def fold_rows(rows, width, first, into):
    n = rows.shape[1]
    count = -(-n // width)
    if count * width > n:
        rows = jnp.concatenate([rows, jnp.zeros((1, count * width - n), rows.dtype)], axis=1)
    at = lax.broadcasted_iota(jnp.int32, into.shape, 0)
    for t in range(count):
        into = jnp.where(at == first + t, rows[:, t * width : (t + 1) * width], into)
    return into, first + count


def fold_ends(left_turned, left, right, width, at, misc):
    count = right.shape[1]
    last = dot(left_turned[width:], right)
    misc, at = fold_rows(last[0:1], width, at, misc)
    rest = count // width * width
    lanes = dot(turn(right[:, rest:])[:TILE], left[:, :width])
    for i in range(count - rest):
        misc, at = fold_rows(lanes[i : i + 1], width, at, misc)
    return misc, at


class Halves:
    def __init__(self, bit, keep, send):
        self.bit, self.keep, self.send = bit, keep, send
        self.half = keep.shape[0]

    def put(self, row, value):
        value = value.astype(BF16)
        for side in (0, 1):
            low, high = max(row, side * self.half), min(row + value.shape[0], (side + 1) * self.half)
            if low >= high:
                continue
            part = value[low - row : high - row]
            at = slice(low - side * self.half, high - side * self.half)

            @pl.when(self.bit == side)
            def _():
                self.keep[at, :] = part

            @pl.when(self.bit != side)
            def _():
                self.send[at, :] = part

    def zero_from(self, row):
        count = 2 * self.half - row
        if count:
            self.put(row, jnp.zeros((count, self.keep.shape[1]), F32))


def first_body(dims, scale, place, *refs):
    share, piece, outs, hidden_units, width = dims
    grads = refs[:share]
    w_decode, gelu, mixed, keep, send, mixed_grad_out, mixed_turned, field_out, turned_grad = refs[share:]
    for d in range(share):
        turned_grad[pl.ds(pl.multiple_of((place[0] ^ d) * piece, TILE), piece), :] = grads[d][...]
    field_t = turned_grad[: up(outs, TILE)]
    field_out[...] = field_t
    packed = Halves(place[1], keep, send)
    field = jnp.swapaxes(field_t.astype(F32), 0, 1).astype(BF16)[:, :outs]
    mixed_grad = dot(field, w_decode[...]).astype(BF16)
    mixed_grad_out[...] = mixed_grad
    mixed_grad_t = turn(mixed_grad)
    mixed_turned[...] = mixed_grad_t
    row = 0
    for part in range(hidden_units // width):
        packed.put(row, dot(mixed_grad_t[:width], gelu[:, part * width : (part + 1) * width]) * scale)
        row += width
    decode_grad = dot(field_t[:outs], mixed[:, :width]) * scale
    if up(outs, TILE) > outs:
        decode_grad = jnp.concatenate([decode_grad, jnp.zeros((up(outs, TILE) - outs, width), F32)], axis=0)
    packed.put(row, decode_grad)
    packed.zero_from(row + up(outs, TILE))


def second_body(dims, scale, place, *refs):
    outs, chans, hidden_units, width, taps_count = dims
    (
        mixed_grad_in, mixed_turned, field_t, w_reduce, w_expand, slopes, hidden, hidden_turned_in, gelu, mixed, spread,
        keep, send, hidden_grad_out, hidden_turned,
    ) = refs
    packed = Halves(place[1], keep, send)
    mixed_grad = mixed_grad_in[...]
    gelu_grad = dot(mixed_grad, w_reduce[...])
    pre_grad = (gelu_grad * slopes[...].astype(F32)).astype(BF16)
    hidden_grad = (mixed_grad.astype(F32) + dot(pre_grad, w_expand[...], 1, 1)).astype(BF16)
    hidden_grad_out[...] = hidden_grad
    hidden_grad_t = turn(hidden_grad)
    hidden_turned[...] = hidden_grad_t
    hidden_t = hidden_turned_in[...]
    row = 0
    for part in range(hidden_units // width):
        packed.put(row, dot(hidden_t[:width], pre_grad[:, part * width : (part + 1) * width]) * scale)
        row += width
    packed.put(row, dot(hidden_grad_t[:width], spread[:, :width]) * scale)
    row += width
    misc = jnp.zeros((misc_height(chans, hidden_units, outs, taps_count, width), width), F32)
    misc, at = fold_ends(hidden_t, hidden[...], pre_grad, width, 0, misc)
    misc, at = fold_ends(mixed_turned[...], mixed_grad, gelu[...], width, at, misc)
    misc, at = fold_ends(hidden_grad_t, hidden_grad, spread[:, :taps_count], width, at, misc)
    tail = dot(turn(mixed[:, width:])[:TILE], field_t[:outs], 1, 1)
    misc, at = fold_rows(tail[0:1], width, at, misc)
    packed.put(row, misc * scale)
    packed.zero_from(row + misc.shape[0])


def misc_height(chans, hidden_units, outs, taps_count, width):
    return up(2 * sum(misc_rows(hidden_units, width)) + sum(misc_rows(taps_count, width)) + 1, TILE)


def third_body(scale, width, place, left, right, keep, send):
    packed = Halves(place[1], keep, send)
    row = 0
    while row < keep.shape[0] * 2 // width * width:
        at = row + width
        packed.put(row, dot(left[:width, :], right[:, at : at + width]) * scale)
        row += width
    packed.zero_from(row)


def bit_of(place, pair):
    return jnp.where(place[1] == 0, place[pair[0]], place[pair[1]])


def combine_body(pair, place, kept, got, send, keep):
    count = keep.shape[0]
    bit = bit_of(place, pair)
    for target, side in ((send, 1 - bit), (keep, bit)):
        rows = pl.ds(pl.multiple_of(side * count, TILE), count)
        target[...] = add_rounded(kept[rows, :], got[rows, :])


class Joined:
    def __init__(self, bit, kept, got):
        self.bit, self.halves = bit, (kept, got)
        self.half = kept.shape[0]

    def parts(self, row, count):
        for side in (0, 1):
            low, high = max(row, side * self.half), min(row + count, (side + 1) * self.half)
            if low < high:
                kept, got = (ref[low - side * self.half : high - side * self.half, :] for ref in self.halves)
                yield low - row, jnp.where(self.bit == side, kept, got)


def put_matrix(out, block_of, misc, at, width):
    count = out.shape[1]
    for part in range(count // width):
        source, row = block_of(part)
        for offset, value in source.parts(row, width):
            out[offset : offset + value.shape[0], part * width : (part + 1) * width] = value
    wide, lanes = misc_rows(count, width)
    rest = count // width * width
    if lanes:
        ends = jnp.swapaxes(misc[at + wide : at + wide + lanes], 0, 1)
        out[:width, rest:] = ends.astype(BF16)
    for t in range(wide):
        size = min(width, count - t * width)
        out[width : width + 1, t * width : t * width + size] = misc[at + t : at + t + 1, :size].astype(BF16)
    return at + wide + lanes


def finish_second_body(dims, place, kept, got, expand_out, misc_out):
    hidden_units, width = dims
    source = Joined(place[1], kept, got)
    for offset, value in source.parts((hidden_units // width + 1) * width, misc_out.shape[0]):
        misc_out[offset : offset + value.shape[0], :] = value
    put_matrix(expand_out, lambda part: (source, part * width), misc_out[...].astype(F32), 0, width)


def finish_first_body(dims, place, kept, got, misc_ref, reduce_out, decode_out):
    hidden_units, outs, taps_count, width = dims
    source = Joined(place[1], kept, got)
    misc = misc_ref[...].astype(F32)
    at = sum(misc_rows(hidden_units, width))
    at = put_matrix(reduce_out, lambda part: (source, part * width), misc, at, width)
    at += sum(misc_rows(taps_count, width))
    for offset, value in source.parts(hidden_units // width * width, outs):
        decode_out[offset : offset + value.shape[0], :width] = value
    turned = jnp.swapaxes(misc[at : at + 8], 0, 1)
    decode_out[:, width:] = turned[:outs, : decode_out.shape[1] - width].astype(BF16)


def finish_third_body(dims, place, kept_second, got_second, kept, got, misc_ref, disco_out):
    hidden_units, width = dims
    second, third = Joined(place[1], kept_second, got_second), Joined(place[1], kept, got)
    first = hidden_units // width * width
    put_matrix(
        disco_out,
        lambda part: (third, (part - 1) * width) if part else (second, first),
        misc_ref[...].astype(F32), 2 * sum(misc_rows(hidden_units, width)), width,
    )


def collect_body(dims, hidden_grad, w_disco, stencil, out, left_out, right_out):
    members, rows, lons, chans, lon_pad, slot, bases = dims
    chan_pad = up(chans, LANES)
    points = rows * lon_pad
    width = chan_pad - LANES
    full = bases * width + LANES
    grad = dot(hidden_grad[...], w_disco[...]).astype(BF16)
    grad = jnp.concatenate([grad, jnp.zeros((grad.shape[0], full - grad.shape[1]), BF16)], axis=1)
    for m in range(members):
        total = None
        for k in range(bases):
            part = dot(stencil[k * points : (k + 1) * points, :], grad[m * points : (m + 1) * points, k * width : k * width + chan_pad], 0, 0)
            part = part if k == 0 else pltpu.roll(part, chan_pad - k, 1)
            total = part if total is None else total + part
        for r in range(rows):
            at = r * slot
            own = hidden_grad[m * points + r * lon_pad : m * points + (r + 1) * lon_pad, :].astype(F32)
            out[m, r] = (own + total[at : at + lon_pad, :chans])[:lons]
            left_out[m, r] = total[at + lon_pad : at + lon_pad + 8, :chans][:reach]
            right_out[m, r] = total[at + lon_pad + 8 : at + lon_pad + 16, :chans][:reach]


def bits_of(axis):
    size, out, bit = lax.axis_size(axis), [], 1
    while bit < size:
        out.append((axis, bit))
        bit *= 2
    return out


def swap(x, pair):
    members, lons = lax.axis_size("member"), lax.axis_size("lon")
    perm = []
    for m in range(members):
        for n in range(lons):
            axis, bit = pair[n % 2]
            to = (m ^ bit) * lons + n if axis == "member" else m * lons + (n ^ bit)
            perm.append((m * lons + n, to))
    return lax.ppermute(x, ("member", "lon"), perm)


def add_rounded(a, b):
    return (a.astype(F32) + b.astype(F32)).astype(BF16)


def streams():
    core, *lon = [(d, d) for d in bits_of("lon")]
    mem = bits_of("member")
    mem = [(d, d) for d in mem]
    orders = [[mem[0], lon[0], lon[1], mem[1]], [lon[0], lon[1], mem[0], mem[1]], [lon[1], mem[0], lon[0], mem[1]]]
    return [[core] + order for order in orders]


def row_unit():
    return 8 * 2 ** (len(streams()[0]) - 1)


def all_dims():
    return bits_of("lon") + bits_of("member")


def places_of(pair):
    return [1 + all_dims().index(dim) for dim in pair]


class Stream:
    def __init__(self, place, keep, send, order):
        self.place, self.kept, self.order = place, keep, order
        self.got = swap(send, order[0])
        self.done = [order[0]]
        self.steps = [self.halve] * (len(order) - 2) + [self.exchange, self.added] + [self.join] * (len(order) - 2)

    def advance(self, last=None):
        if last is not None and last is not self:
            self.got, last.kept = lax.optimization_barrier((self.got, last.kept))
        self.steps.pop(0)()
        return self

    def halve(self):
        pair = self.order[len(self.done)]
        count, at = self.kept.shape[0] // 2, places_of(pair)
        if count % TILE == 0 and len(self.done) < 3:
            shape = ((count, self.kept.shape[1]), BF16)
            args = [self.place, self.kept, self.got]
            send, keep = vmem_call(functools.partial(combine_body, at), [shape] * 2, args, smem=1, name="combine")
        else:
            bit = bit_of(self.place, at)
            send, keep = (
                add_rounded(*(lax.dynamic_slice_in_dim(x, side * count, count, axis=0) for x in (self.kept, self.got)))
                for side in (1 - bit, bit)
            )
        self.got, self.kept = swap(send, pair), keep
        self.done.append(pair)

    def exchange(self):
        self.kept = add_rounded(self.kept, self.got)
        self.got = swap(self.kept, self.order[-1])

    def added(self):
        self.kept = add_rounded(self.kept, self.got)
        self.send_back()

    def join(self):
        low = bit_of(self.place, places_of(self.done.pop())) == 0
        self.kept = jnp.concatenate([jnp.where(low, self.kept, self.got), jnp.where(low, self.got, self.kept)], axis=0)
        self.send_back()

    def send_back(self):
        self.got = swap(self.kept, self.done[-1])


def shifted(x, axis, by):
    size = lax.axis_size(axis)
    return lax.ppermute(x, axis, [(i, (i + by) % size) for i in range(size)])


def exchanged(piece_of, axis):
    size = lax.axis_size(axis)
    return [piece_of(0)] + [lax.ppermute(piece_of(d), axis, [(i, i ^ d) for i in range(size)]) for d in range(1, size)]


def per_device(
    latent, member_seeds, member_table, row_bands, disco_basis, w_disco, w_expand, w_reduce, w_decode, target
):
    members, rows, lons, chans = latent.shape
    bases = disco_basis.shape[1]
    hidden_units = w_expand.shape[1]
    outs = w_decode.shape[1]
    share = lax.axis_size("member")
    total_members = members * share
    lon_pad = up(lons, TILE)
    slot = lon_pad + TILE
    points = rows * lon_pad
    flat = members * points
    width = chans // LANES * LANES
    full = bases * width + LANES
    piece = TILE * -(-up(outs, TILE) // (TILE * share))
    me = lax.axis_index("member")
    place = jnp.stack([me] + [lax.axis_index(axis) // bit % 2 for axis, bit in all_dims()]).astype(jnp.int32)
    by_lon = jnp.swapaxes(latent, 1, 2)
    left = jnp.swapaxes(shifted(by_lon[:, lons - reach :], "lon", 1), 1, 2)
    right = jnp.swapaxes(shifted(by_lon[:, :reach], "lon", -1), 1, 2)
    disco_t, reduce_t, decode_t = w_disco.T, w_reduce.T, w_decode.T
    dims = (members, rows, lons, chans, lon_pad, slot, bases, piece, share)
    stencil, offsets = vmem_call(
        functools.partial(prepare_body, dims),
        [((bases * points, rows * slot), BF16), ((TILE, chans), F32)],
        [member_seeds, row_bands, disco_basis.astype(F32).reshape(-1), member_table],
        smem=3,
        name="prepare",
        moved=4 * 2**20,
    )
    spread, hidden, gelu, pre = vmem_call(
        functools.partial(forward_body, dims),
        [((flat, full), BF16), ((flat, chans), BF16), ((flat, hidden_units), BF16), ((flat, hidden_units), F32)],
        [place, latent, left, right, stencil, offsets, disco_t, w_expand],
        smem=1,
        scratch=[pltpu.VMEM((members, rows * slot, up(chans, LANES)), F32)],
        name="forward",
        moved=24 * 2**20,
    )
    mixed, *here = vmem_call(
        functools.partial(fields_body, dims),
        [((flat, chans), BF16)] + [((piece, flat), BF16)] * share,
        [place, hidden, gelu, reduce_t, decode_t],
        smem=1,
        scratch=[pltpu.VMEM((share * piece, flat), BF16)],
        name="fields",
        moved=6 * 2**20,
    )
    turned_shape = ((up(chans, TILE), flat), BF16)
    slopes, input_turned = vmem_call(
        slopes_body, [((flat, hidden_units), BF16), turned_shape], [pre, hidden], name="slopes"
    )
    here_out = here
    observed = jnp.pad(target, ((0, 0), (0, lon_pad - lons), (0, share * piece - outs))).reshape(points, share * piece).T
    observed = jnp.concatenate([observed] * members, axis=1)
    observed = lax.dynamic_slice_in_dim(observed, me * piece, piece, axis=0)
    here = exchanged(lambda d: here_out[d], "member")
    observed, slopes, input_turned = lax.optimization_barrier((observed, slopes, input_turned))
    grads = vmem_call(
        functools.partial(crps_body, share, points, members, total_members),
        [((piece, flat), BF16)] * share,
        here + [observed],
        name="crps",
        moved=3 * 2**20,
    )
    back = exchanged(lambda d: grads[d], "member")
    scale = 1.0 / math.sqrt(total_members * rows * lons * lax.axis_size("lon"))
    unit = row_unit()
    taps_count = bases * chans
    orders = streams()

    def halves(rows):
        return [((up(rows, unit) // 2, width), BF16)] * 2

    blocks = hidden_units // width
    keep, send, mixed_grad, mixed_turned, field_turned = vmem_call(
        functools.partial(first_body, (share, piece, outs, hidden_units, width), scale),
        halves(blocks * width + up(outs, TILE)) + [((flat, chans), BF16), turned_shape, ((up(outs, TILE), flat), BF16)],
        [place] + back + [decode_t, gelu, mixed],
        smem=1,
        scratch=[pltpu.VMEM((share * piece, flat), BF16)],
        name="first_products",
        moved=9 * 2**20,
    )
    first = Stream(place, keep, send, orders[0])
    misc_shape = ((misc_height(chans, hidden_units, outs, taps_count, width), width), BF16)
    keep, send, hidden_grad, hidden_turned = vmem_call(
        functools.partial(second_body, (outs, chans, hidden_units, width, taps_count), scale),
        halves((blocks + 1) * width + misc_shape[0][0]) + [((flat, chans), BF16), turned_shape],
        [place, mixed_grad, mixed_turned, field_turned, reduce_t, w_expand, slopes, hidden, input_turned, gelu, mixed, spread],
        smem=1,
        name="second_products",
    )
    second = Stream(place, keep, send, orders[1])
    first.advance()
    hidden_turned, first.kept = lax.optimization_barrier((hidden_turned, first.kept))
    keep, send = vmem_call(
        functools.partial(third_body, scale, width),
        halves((taps_count // width - 1) * width),
        [place, hidden_turned, spread],
        smem=1,
        name="third_products",
    )
    third = Stream(place, keep, send, orders[2])
    second.advance()
    last = third.advance(second)
    hidden_grad, third.kept = lax.optimization_barrier((hidden_grad, third.kept))
    dims = (members, rows, lons, chans, lon_pad, slot, bases)
    latent_grad, to_left, to_right = vmem_call(
        functools.partial(collect_body, dims),
        [(latent.shape, F32), ((members, rows, reach, chans), F32), ((members, rows, reach, chans), F32)],
        [hidden_grad, disco_t, stencil],
        name="collect",
    )
    first.got, latent_grad = lax.optimization_barrier((first.got, latent_grad))
    from_right = shifted(to_left, "lon", -1)
    from_left = shifted(to_right, "lon", 1)
    for stream in (first, second, third) * 4:
        last = stream.advance(last)
    first.got, from_right, from_left = lax.optimization_barrier((first.got, from_right, from_left))
    edge = [(0, 0, 0)] * 2
    latent_grad = (
        latent_grad
        + lax.pad(from_right, jnp.float32(0), edge + [(lons - reach, 0, 0), (0, 0, 0)])
        + lax.pad(from_left, jnp.float32(0), edge + [(0, lons - reach, 0), (0, 0, 0)])
    ).astype(BF16)

    latent_grad = with_layout_constraint(jnp.swapaxes(latent_grad, 1, 2), Layout(major_to_minor=(0, 1, 2, 3)))
    for stream in (first, second, third):
        last = stream.advance(last)
    first.got, latent_grad = lax.optimization_barrier((first.got, latent_grad))
    while third.steps:
        for stream in (first, second, third):
            if stream.steps:
                last = stream.advance(last)
    grad_expand, misc = vmem_call(
        functools.partial(finish_second_body, (hidden_units, width)),
        [(w_expand.shape, BF16), misc_shape],
        [place, second.kept, second.got],
        smem=1,
        name="finish_second",
    )
    reduce_grad_t, decode_grad_t = vmem_call(
        functools.partial(finish_first_body, (hidden_units, outs, taps_count, width)),
        [(reduce_t.shape, BF16), (decode_t.shape, BF16)],
        [place, first.kept, first.got, misc],
        smem=1,
        name="finish_first",
    )
    (disco_grad_t,) = vmem_call(
        functools.partial(finish_third_body, (hidden_units, width)),
        [(disco_t.shape, BF16)],
        [place, second.kept, second.got, third.kept, third.got, misc],
        smem=1,
        name="finish_third",
    )
    return jnp.swapaxes(latent_grad, 1, 2), disco_grad_t.T, grad_expand, reduce_grad_t.T, decode_grad_t.T


def solution(mesh):
    placed = (
        P("member", None, "lon", None),
        P("member"),
        P(),
        P(),
        P(),
        P(),
        P(),
        P(),
        P(),
        P(None, "lon", None),
    )
    return jax.shard_map(
        per_device,
        mesh=mesh,
        in_specs=placed,
        out_specs=(P("member", None, "lon", None), P(), P(), P(), P()),
        check_vma=False,
    )
```

```python
import functools
import math

import jax
import jax.numpy as jnp
from jax import lax
from jax.experimental import pallas as pl
from jax.experimental.layout import Layout, with_layout_constraint
from jax.experimental.pallas import tpu as pltpu
from jax.sharding import PartitionSpec as P

reach = 3
taps = 2 * reach + 1
smooth = 0.5
LANES = 128
TILE = 16
VMEM_LIMIT = 24 * 2**20
F32 = jnp.float32
BF16 = jnp.bfloat16


def up(value, unit):
    return -(-value // unit) * unit


def dot(a, b, ca=1, cb=0):
    return lax.dot_general(a, b, (((ca,), (cb,)), ((), ())), preferred_element_type=F32)


def slope(d):
    return d * lax.rsqrt(d * d + smooth * smooth)


def vmem_call(body, outs, args, smem=0, scratch=(), name=None, moved=0):
    specs = [pl.BlockSpec(memory_space=pltpu.SMEM)] * smem
    specs += [pl.BlockSpec(memory_space=pltpu.VMEM)] * (len(args) - smem)
    return pl.pallas_call(
        body,
        out_shape=[jax.ShapeDtypeStruct(shape, dtype) for shape, dtype in outs],
        in_specs=specs,
        out_specs=[pl.BlockSpec(memory_space=pltpu.VMEM)] * len(outs),
        scratch_shapes=list(scratch),
        compiler_params=pltpu.CompilerParams(vmem_limit_bytes=VMEM_LIMIT),
        cost_estimate=pl.CostEstimate(flops=0, bytes_accessed=moved, transcendentals=0),
        name=name,
    )(*args)


def prepare_body(dims, seeds, bands, basis, table, stencil_out, offsets_out):
    members, rows, lons, chans, lon_pad, slot, bases, piece, share = dims
    points = rows * lon_pad
    per_tile = LANES // slot
    lane = lax.broadcasted_iota(jnp.int32, (lon_pad, LANES), 1)
    lon = lax.broadcasted_iota(jnp.int32, (lon_pad, LANES), 0)
    place = lane % slot
    own = place < lons
    before = (place >= lon_pad) & (place < lon_pad + reach)
    after = (place >= lon_pad + 8) & (place < lon_pad + 8 + reach)
    wide_lon = jnp.where(own, place + reach, jnp.where(before, place - lon_pad, place - lon_pad - 8 + lons + reach))
    tap = jnp.where((own | before | after) & (lon < lons), wide_lon - lon, -1)
    tap = jnp.where(lane < slot, tap, tap + 1000 * (lane // slot))
    masks = [[tap == 1000 * part + b for b in range(taps)] for part in range(per_tile)]
    for r in range(rows):
        band = bands[r]
        for k in range(bases):
            for t in range(rows // per_tile):
                block = jnp.zeros((lon_pad, LANES), F32)
                for part in range(per_tile):
                    a = t * per_tile + part - r + reach
                    if not 0 <= a < taps:
                        continue
                    base = ((band * bases + k) * taps + a) * taps
                    for b in range(taps):
                        block = jnp.where(masks[part][b], basis[base + b], block)
                stencil_out[k * points + r * lon_pad : k * points + (r + 1) * lon_pad, t * LANES : (t + 1) * LANES] = block.astype(BF16)
    seed_count = table.shape[0]
    mrow = lax.broadcasted_iota(jnp.int32, (TILE, seed_count), 0)
    mcol = lax.broadcasted_iota(jnp.int32, (TILE, seed_count), 1)
    onehot = jnp.zeros((TILE, seed_count), F32)
    for m in range(members):
        onehot = jnp.where((mrow == m) & (mcol == seeds[m]), 1.0, onehot)
    offsets_out[...] = dot(onehot.astype(BF16), table[...])


def forward_body(
    dims, place, latent, left, right, stencil, offsets_in, w_disco, w_expand, *refs
):
    members, rows, lons, chans, lon_pad, slot, bases, piece, share = dims
    spread_out, hidden_out, gelu_out, pre_out, wide = refs
    chan_pad = up(chans, LANES)
    points = rows * lon_pad
    offsets = offsets_in[...]
    wide[...] = jnp.zeros_like(wide)
    for m in range(members):
        off = offsets[m : m + 1, :]
        for r in range(rows):
            for ref, start, count in ((latent, 0, lons), (left, lon_pad, reach), (right, lon_pad + 8, reach)):
                seeded = (ref[m, r].astype(F32) + off).astype(BF16).astype(F32)
                wide[m, r * slot + start : r * slot + start + count, :chans] = seeded
    for m in range(members):
        full = wide[m]
        carry = None
        for k in range(bases):
            moved = full if k == 0 else pltpu.roll(full, k, 1)
            out = dot(stencil[k * points : (k + 1) * points, :], moved.astype(BF16))
            width = chan_pad - LANES
            first = out[:, :LANES] if carry is None else out[:, :LANES] + carry
            rows_here = slice(m * points, (m + 1) * points)
            spread_out[rows_here, k * width : k * width + LANES] = first.astype(BF16)
            spread_out[rows_here, k * width + LANES : (k + 1) * width] = out[:, LANES:width].astype(BF16)
            carry = out[:, width:]
        spread_out[rows_here, bases * width : bases * width + LANES] = carry.astype(BF16)
    seeded_rows = jnp.concatenate(
        [wide[m, r * slot : r * slot + lon_pad, :chans] for m in range(members) for r in range(rows)], axis=0
    )
    conv = dot(spread_out[:, : bases * chans], w_disco[...], 1, 1)
    hidden = (seeded_rows + conv).astype(BF16)
    hidden_out[...] = hidden
    pre = dot(hidden, w_expand[...])
    rate = math.sqrt(2.0 / math.pi)
    square = pre * pre
    th = jnp.tanh(rate * (pre + 0.044715 * (square * pre)))
    half = 0.5 * (1.0 + th)
    act = (pre * half).astype(BF16)
    gelu_out[...] = act
    pre_out[...] = pre


def fields_body(dims, place, hidden_in, act, w_reduce, w_decode, *refs):
    members, rows, lons, chans, lon_pad, slot, bases, piece, share = dims
    mixed_out, fields_out, turned_fields = refs[0], refs[1 : 1 + share], refs[1 + share]
    hidden = hidden_in[...]
    mixed = (hidden.astype(F32) + dot(act[...], w_reduce[...], 1, 1)).astype(BF16)
    mixed_out[...] = mixed
    turned = dot(w_decode[...], mixed, 1, 1).astype(BF16)
    outs = turned.shape[0]
    if share * piece > outs:
        turned = jnp.concatenate([turned, jnp.zeros((share * piece - outs, turned.shape[1]), BF16)], axis=0)
    turned_fields[...] = turned
    for d in range(share):
        fields_out[d][...] = turned_fields[pl.ds(pl.multiple_of((place[0] ^ d) * piece, TILE), piece), :]


def slopes_body(pre_in, hidden, slope_out, hidden_turned):
    rate = math.sqrt(2.0 / math.pi)
    pre = pre_in[...]
    square = pre * pre
    th = jnp.tanh(rate * (pre + 0.044715 * (square * pre)))
    half = 0.5 * (1.0 + th)
    slope_out[...] = (half + 0.5 * pre * (1.0 - th * th) * (rate * (1.0 + 3 * 0.044715 * square))).astype(BF16)
    hidden_turned[...] = turn(hidden[...])


def crps_body(count, points, members, total, *refs):
    fields = [ref[...].astype(F32) for ref in refs[:count]]
    observed = refs[count][...].astype(F32)
    outs = refs[count + 1 :]
    turned = [[f] + [pltpu.roll(f, t * points, 1) for t in range(1, members)] for f in fields]
    for i in range(count):
        paired = jnp.zeros_like(observed)
        for j in range(count):
            for t in range(members):
                if i == j and t == 0:
                    continue
                paired = paired + slope(fields[i] - turned[j][t])
        outs[i][...] = (slope(fields[i] - observed) - paired * (1.0 / (total - 1))).astype(BF16)


def turn(x):
    n, c = x.shape
    wide = jnp.concatenate([x.astype(F32), jnp.zeros((n, up(c, LANES) - c), F32)], axis=1)
    return jnp.swapaxes(wide, 0, 1)[: up(c, TILE)].astype(BF16)


def misc_rows(count, width):
    return -(-count // width), count - count // width * width


def fold_rows(rows, width, first, into):
    n = rows.shape[1]
    count = -(-n // width)
    if count * width > n:
        rows = jnp.concatenate([rows, jnp.zeros((1, count * width - n), rows.dtype)], axis=1)
    at = lax.broadcasted_iota(jnp.int32, into.shape, 0)
    for t in range(count):
        into = jnp.where(at == first + t, rows[:, t * width : (t + 1) * width], into)
    return into, first + count


def fold_ends(left_turned, left, right, width, at, misc):
    count = right.shape[1]
    last = dot(left_turned[width:], right)
    misc, at = fold_rows(last[0:1], width, at, misc)
    rest = count // width * width
    lanes = dot(turn(right[:, rest:])[:TILE], left[:, :width])
    for i in range(count - rest):
        misc, at = fold_rows(lanes[i : i + 1], width, at, misc)
    return misc, at


class Halves:
    def __init__(self, bit, keep, send):
        self.bit, self.keep, self.send = bit, keep, send
        self.half = keep.shape[0]

    def put(self, row, value):
        value = value.astype(BF16)
        for side in (0, 1):
            low, high = max(row, side * self.half), min(row + value.shape[0], (side + 1) * self.half)
            if low >= high:
                continue
            part = value[low - row : high - row]
            at = slice(low - side * self.half, high - side * self.half)

            @pl.when(self.bit == side)
            def _():
                self.keep[at, :] = part

            @pl.when(self.bit != side)
            def _():
                self.send[at, :] = part

    def zero_from(self, row):
        count = 2 * self.half - row
        if count:
            self.put(row, jnp.zeros((count, self.keep.shape[1]), F32))


def first_body(dims, scale, place, *refs):
    share, piece, outs, hidden_units, width = dims
    grads = refs[:share]
    w_decode, gelu, mixed, keep, send, mixed_grad_out, mixed_turned, field_out, turned_grad = refs[share:]
    for d in range(share):
        turned_grad[pl.ds(pl.multiple_of((place[0] ^ d) * piece, TILE), piece), :] = grads[d][...]
    field_t = turned_grad[: up(outs, TILE)]
    field_out[...] = field_t
    packed = Halves(place[1], keep, send)
    field = jnp.swapaxes(field_t.astype(F32), 0, 1).astype(BF16)[:, :outs]
    mixed_grad = dot(field, w_decode[...]).astype(BF16)
    mixed_grad_out[...] = mixed_grad
    mixed_grad_t = turn(mixed_grad)
    mixed_turned[...] = mixed_grad_t
    row = 0
    for part in range(hidden_units // width):
        packed.put(row, dot(mixed_grad_t[:width], gelu[:, part * width : (part + 1) * width]) * scale)
        row += width
    decode_grad = dot(field_t[:outs], mixed[:, :width]) * scale
    if up(outs, TILE) > outs:
        decode_grad = jnp.concatenate([decode_grad, jnp.zeros((up(outs, TILE) - outs, width), F32)], axis=0)
    packed.put(row, decode_grad)
    packed.zero_from(row + up(outs, TILE))


def second_body(dims, scale, place, *refs):
    outs, chans, hidden_units, width, taps_count = dims
    (
        mixed_grad_in, mixed_turned, field_t, w_reduce, w_expand, slopes, hidden, hidden_turned_in, gelu, mixed, spread,
        keep, send, hidden_grad_out, hidden_turned,
    ) = refs
    packed = Halves(place[1], keep, send)
    mixed_grad = mixed_grad_in[...]
    gelu_grad = dot(mixed_grad, w_reduce[...])
    pre_grad = (gelu_grad * slopes[...].astype(F32)).astype(BF16)
    hidden_grad = (mixed_grad.astype(F32) + dot(pre_grad, w_expand[...], 1, 1)).astype(BF16)
    hidden_grad_out[...] = hidden_grad
    hidden_grad_t = turn(hidden_grad)
    hidden_turned[...] = hidden_grad_t
    hidden_t = hidden_turned_in[...]
    row = 0
    for part in range(hidden_units // width):
        packed.put(row, dot(hidden_t[:width], pre_grad[:, part * width : (part + 1) * width]) * scale)
        row += width
    packed.put(row, dot(hidden_grad_t[:width], spread[:, :width]) * scale)
    row += width
    misc = jnp.zeros((misc_height(chans, hidden_units, outs, taps_count, width), width), F32)
    misc, at = fold_ends(hidden_t, hidden[...], pre_grad, width, 0, misc)
    misc, at = fold_ends(mixed_turned[...], mixed_grad, gelu[...], width, at, misc)
    misc, at = fold_ends(hidden_grad_t, hidden_grad, spread[:, :taps_count], width, at, misc)
    tail = dot(turn(mixed[:, width:])[:TILE], field_t[:outs], 1, 1)
    misc, at = fold_rows(tail[0:1], width, at, misc)
    packed.put(row, misc * scale)
    packed.zero_from(row + misc.shape[0])


def misc_height(chans, hidden_units, outs, taps_count, width):
    return up(2 * sum(misc_rows(hidden_units, width)) + sum(misc_rows(taps_count, width)) + 1, TILE)


def third_body(scale, width, place, left, right, keep, send):
    packed = Halves(place[1], keep, send)
    row = 0
    while row < keep.shape[0] * 2 // width * width:
        at = row + width
        packed.put(row, dot(left[:width, :], right[:, at : at + width]) * scale)
        row += width
    packed.zero_from(row)


def bit_of(place, pair):
    return jnp.where(place[1] == 0, place[pair[0]], place[pair[1]])


def combine_body(pair, place, kept, got, send, keep):
    count = keep.shape[0]
    bit = bit_of(place, pair)
    for target, side in ((send, 1 - bit), (keep, bit)):
        rows = pl.ds(pl.multiple_of(side * count, TILE), count)
        target[...] = add_rounded(kept[rows, :], got[rows, :])


class Joined:
    def __init__(self, bit, kept, got):
        self.bit, self.halves = bit, (kept, got)
        self.half = kept.shape[0]

    def parts(self, row, count):
        for side in (0, 1):
            low, high = max(row, side * self.half), min(row + count, (side + 1) * self.half)
            if low < high:
                kept, got = (ref[low - side * self.half : high - side * self.half, :] for ref in self.halves)
                yield low - row, jnp.where(self.bit == side, kept, got)


def put_matrix(out, block_of, misc, at, width):
    count = out.shape[1]
    for part in range(count // width):
        source, row = block_of(part)
        for offset, value in source.parts(row, width):
            out[offset : offset + value.shape[0], part * width : (part + 1) * width] = value
    wide, lanes = misc_rows(count, width)
    rest = count // width * width
    if lanes:
        ends = jnp.swapaxes(misc[at + wide : at + wide + lanes], 0, 1)
        out[:width, rest:] = ends.astype(BF16)
    for t in range(wide):
        size = min(width, count - t * width)
        out[width : width + 1, t * width : t * width + size] = misc[at + t : at + t + 1, :size].astype(BF16)
    return at + wide + lanes


def finish_second_body(dims, place, kept, got, expand_out, misc_out):
    hidden_units, width = dims
    source = Joined(place[1], kept, got)
    for offset, value in source.parts((hidden_units // width + 1) * width, misc_out.shape[0]):
        misc_out[offset : offset + value.shape[0], :] = value
    put_matrix(expand_out, lambda part: (source, part * width), misc_out[...].astype(F32), 0, width)


def finish_rest_body(dims, place, kept, got, kept_second, got_second, kept_third, got_third, misc_ref, reduce_out, decode_out, disco_out):
    hidden_units, outs, taps_count, width = dims
    first, second = Joined(place[1], kept, got), Joined(place[1], kept_second, got_second)
    third = Joined(place[1], kept_third, got_third)
    misc = misc_ref[...].astype(F32)
    base = hidden_units // width * width
    at = sum(misc_rows(hidden_units, width))
    at = put_matrix(reduce_out, lambda part: (first, part * width), misc, at, width)
    at = put_matrix(disco_out, lambda part: (third, (part - 1) * width) if part else (second, base), misc, at, width)
    for offset, value in first.parts(base, outs):
        decode_out[offset : offset + value.shape[0], :width] = value
    turned = jnp.swapaxes(misc[at : at + 8], 0, 1)
    decode_out[:, width:] = turned[:outs, : decode_out.shape[1] - width].astype(BF16)


def collect_body(dims, hidden_grad, w_disco, stencil, out, left_out, right_out):
    members, rows, lons, chans, lon_pad, slot, bases = dims
    chan_pad = up(chans, LANES)
    points = rows * lon_pad
    width = chan_pad - LANES
    full = bases * width + LANES
    grad = dot(hidden_grad[...], w_disco[...]).astype(BF16)
    grad = jnp.concatenate([grad, jnp.zeros((grad.shape[0], full - grad.shape[1]), BF16)], axis=1)
    for m in range(members):
        total = None
        for k in range(bases):
            part = dot(stencil[k * points : (k + 1) * points, :], grad[m * points : (m + 1) * points, k * width : k * width + chan_pad], 0, 0)
            part = part if k == 0 else pltpu.roll(part, chan_pad - k, 1)
            total = part if total is None else total + part
        for r in range(rows):
            at = r * slot
            own = hidden_grad[m * points + r * lon_pad : m * points + (r + 1) * lon_pad, :].astype(F32)
            out[m, r] = (own + total[at : at + lon_pad, :chans])[:lons]
            left_out[m, r] = total[at + lon_pad : at + lon_pad + 8, :chans][:reach]
            right_out[m, r] = total[at + lon_pad + 8 : at + lon_pad + 16, :chans][:reach]


def bits_of(axis):
    size, out, bit = lax.axis_size(axis), [], 1
    while bit < size:
        out.append((axis, bit))
        bit *= 2
    return out


def swap(x, pair):
    members, lons = lax.axis_size("member"), lax.axis_size("lon")
    perm = []
    for m in range(members):
        for n in range(lons):
            axis, bit = pair[n % 2]
            to = (m ^ bit) * lons + n if axis == "member" else m * lons + (n ^ bit)
            perm.append((m * lons + n, to))
    return lax.ppermute(x, ("member", "lon"), perm)


def add_rounded(a, b):
    return (a.astype(F32) + b.astype(F32)).astype(BF16)


def streams():
    core, *lon = [(d, d) for d in bits_of("lon")]
    mem = bits_of("member")
    mem = [(d, d) for d in mem]
    orders = [[mem[0], lon[0], lon[1], mem[1]], [lon[0], lon[1], mem[0], mem[1]], [lon[1], mem[0], lon[0], mem[1]]]
    return [[core] + order for order in orders]


def row_unit():
    return 8 * 2 ** (len(streams()[0]) - 1)


def all_dims():
    return bits_of("lon") + bits_of("member")


def places_of(pair):
    return [1 + all_dims().index(dim) for dim in pair]


class Stream:
    def __init__(self, place, keep, send, order):
        self.place, self.kept, self.order = place, keep, order
        self.got = swap(send, order[0])
        self.done = [order[0]]
        self.steps = [self.halve] * (len(order) - 2) + [self.exchange, self.added] + [self.join] * (len(order) - 2)

    def advance(self, last=None):
        if last is not None and last is not self:
            self.got, last.kept = lax.optimization_barrier((self.got, last.kept))
        self.steps.pop(0)()
        return self

    def halve(self):
        pair = self.order[len(self.done)]
        count, at = self.kept.shape[0] // 2, places_of(pair)
        if count % TILE == 0 and len(self.done) < 3:
            shape = ((count, self.kept.shape[1]), BF16)
            args = [self.place, self.kept, self.got]
            send, keep = vmem_call(functools.partial(combine_body, at), [shape] * 2, args, smem=1, name="combine")
        else:
            bit = bit_of(self.place, at)
            send, keep = (
                add_rounded(*(lax.dynamic_slice_in_dim(x, side * count, count, axis=0) for x in (self.kept, self.got)))
                for side in (1 - bit, bit)
            )
        self.got, self.kept = swap(send, pair), keep
        self.done.append(pair)

    def exchange(self):
        self.kept = add_rounded(self.kept, self.got)
        self.got = swap(self.kept, self.order[-1])

    def added(self):
        self.kept = add_rounded(self.kept, self.got)
        self.send_back()

    def join(self):
        low = bit_of(self.place, places_of(self.done.pop())) == 0
        self.kept = jnp.concatenate([jnp.where(low, self.kept, self.got), jnp.where(low, self.got, self.kept)], axis=0)
        self.send_back()

    def send_back(self):
        self.got = swap(self.kept, self.done[-1])


def shifted(x, axis, by):
    size = lax.axis_size(axis)
    return lax.ppermute(x, axis, [(i, (i + by) % size) for i in range(size)])


def exchanged(piece_of, axis):
    size = lax.axis_size(axis)
    return [piece_of(0)] + [lax.ppermute(piece_of(d), axis, [(i, i ^ d) for i in range(size)]) for d in range(1, size)]


def per_device(
    latent, member_seeds, member_table, row_bands, disco_basis, w_disco, w_expand, w_reduce, w_decode, target
):
    members, rows, lons, chans = latent.shape
    bases = disco_basis.shape[1]
    hidden_units = w_expand.shape[1]
    outs = w_decode.shape[1]
    share = lax.axis_size("member")
    total_members = members * share
    lon_pad = up(lons, TILE)
    slot = lon_pad + TILE
    points = rows * lon_pad
    flat = members * points
    width = chans // LANES * LANES
    full = bases * width + LANES
    piece = TILE * -(-up(outs, TILE) // (TILE * share))
    me = lax.axis_index("member")
    place = jnp.stack([me] + [lax.axis_index(axis) // bit % 2 for axis, bit in all_dims()]).astype(jnp.int32)
    by_lon = jnp.swapaxes(latent, 1, 2)
    left = jnp.swapaxes(shifted(by_lon[:, lons - reach :], "lon", 1), 1, 2)
    right = jnp.swapaxes(shifted(by_lon[:, :reach], "lon", -1), 1, 2)
    disco_t, reduce_t, decode_t = w_disco.T, w_reduce.T, w_decode.T
    dims = (members, rows, lons, chans, lon_pad, slot, bases, piece, share)
    stencil, offsets = vmem_call(
        functools.partial(prepare_body, dims),
        [((bases * points, rows * slot), BF16), ((TILE, chans), F32)],
        [member_seeds, row_bands, disco_basis.astype(F32).reshape(-1), member_table],
        smem=3,
        name="prepare",
        moved=4 * 2**20,
    )
    spread, hidden, gelu, pre = vmem_call(
        functools.partial(forward_body, dims),
        [((flat, full), BF16), ((flat, chans), BF16), ((flat, hidden_units), BF16), ((flat, hidden_units), F32)],
        [place, latent, left, right, stencil, offsets, disco_t, w_expand],
        smem=1,
        scratch=[pltpu.VMEM((members, rows * slot, up(chans, LANES)), F32)],
        name="forward",
        moved=24 * 2**20,
    )
    mixed, *here = vmem_call(
        functools.partial(fields_body, dims),
        [((flat, chans), BF16)] + [((piece, flat), BF16)] * share,
        [place, hidden, gelu, reduce_t, decode_t],
        smem=1,
        scratch=[pltpu.VMEM((share * piece, flat), BF16)],
        name="fields",
        moved=6 * 2**20,
    )
    turned_shape = ((up(chans, TILE), flat), BF16)
    slopes, input_turned = vmem_call(
        slopes_body, [((flat, hidden_units), BF16), turned_shape], [pre, hidden], name="slopes"
    )
    here_out = here
    observed = jnp.pad(target, ((0, 0), (0, lon_pad - lons), (0, share * piece - outs))).reshape(points, share * piece).T
    observed = jnp.concatenate([observed] * members, axis=1)
    observed = lax.dynamic_slice_in_dim(observed, me * piece, piece, axis=0)
    here = exchanged(lambda d: here_out[d], "member")
    observed, slopes, input_turned = lax.optimization_barrier((observed, slopes, input_turned))
    grads = vmem_call(
        functools.partial(crps_body, share, points, members, total_members),
        [((piece, flat), BF16)] * share,
        here + [observed],
        name="crps",
        moved=3 * 2**20,
    )
    back = exchanged(lambda d: grads[d], "member")
    scale = 1.0 / math.sqrt(total_members * rows * lons * lax.axis_size("lon"))
    unit = row_unit()
    taps_count = bases * chans
    orders = streams()

    def halves(rows):
        return [((up(rows, unit) // 2, width), BF16)] * 2

    blocks = hidden_units // width
    keep, send, mixed_grad, mixed_turned, field_turned = vmem_call(
        functools.partial(first_body, (share, piece, outs, hidden_units, width), scale),
        halves(blocks * width + up(outs, TILE)) + [((flat, chans), BF16), turned_shape, ((up(outs, TILE), flat), BF16)],
        [place] + back + [decode_t, gelu, mixed],
        smem=1,
        scratch=[pltpu.VMEM((share * piece, flat), BF16)],
        name="first_products",
        moved=9 * 2**20,
    )
    first = Stream(place, keep, send, orders[0])
    misc_shape = ((misc_height(chans, hidden_units, outs, taps_count, width), width), BF16)
    keep, send, hidden_grad, hidden_turned = vmem_call(
        functools.partial(second_body, (outs, chans, hidden_units, width, taps_count), scale),
        halves((blocks + 1) * width + misc_shape[0][0]) + [((flat, chans), BF16), turned_shape],
        [place, mixed_grad, mixed_turned, field_turned, reduce_t, w_expand, slopes, hidden, input_turned, gelu, mixed, spread],
        smem=1,
        name="second_products",
    )
    second = Stream(place, keep, send, orders[1])
    first.advance()
    hidden_turned, first.kept = lax.optimization_barrier((hidden_turned, first.kept))
    keep, send = vmem_call(
        functools.partial(third_body, scale, width),
        halves((taps_count // width - 1) * width),
        [place, hidden_turned, spread],
        smem=1,
        name="third_products",
    )
    third = Stream(place, keep, send, orders[2])
    second.advance()
    last = third.advance(second)
    hidden_grad, third.kept = lax.optimization_barrier((hidden_grad, third.kept))
    dims = (members, rows, lons, chans, lon_pad, slot, bases)
    latent_grad, to_left, to_right = vmem_call(
        functools.partial(collect_body, dims),
        [(latent.shape, F32), ((members, rows, reach, chans), F32), ((members, rows, reach, chans), F32)],
        [hidden_grad, disco_t, stencil],
        name="collect",
    )
    first.got, latent_grad = lax.optimization_barrier((first.got, latent_grad))
    from_right = shifted(to_left, "lon", -1)
    from_left = shifted(to_right, "lon", 1)
    for stream in (first, second, third) * 4:
        last = stream.advance(last)
    first.got, from_right, from_left = lax.optimization_barrier((first.got, from_right, from_left))
    edge = [(0, 0, 0)] * 2
    latent_grad = (
        latent_grad
        + lax.pad(from_right, jnp.float32(0), edge + [(lons - reach, 0, 0), (0, 0, 0)])
        + lax.pad(from_left, jnp.float32(0), edge + [(0, lons - reach, 0), (0, 0, 0)])
    ).astype(BF16)

    latent_grad = with_layout_constraint(jnp.swapaxes(latent_grad, 1, 2), Layout(major_to_minor=(0, 1, 2, 3)))
    for stream in (first, second, third):
        last = stream.advance(last)
    first.got, latent_grad = lax.optimization_barrier((first.got, latent_grad))
    while third.steps:
        for stream in (first, second, third):
            if stream.steps:
                last = stream.advance(last)
    grad_expand, misc = vmem_call(
        functools.partial(finish_second_body, (hidden_units, width)),
        [(w_expand.shape, BF16), misc_shape],
        [place, second.kept, second.got],
        smem=1,
        name="finish_second",
    )
    reduce_grad_t, decode_grad_t, disco_grad_t = vmem_call(
        functools.partial(finish_rest_body, (hidden_units, outs, taps_count, width)),
        [(reduce_t.shape, BF16), (decode_t.shape, BF16), (disco_t.shape, BF16)],
        [place, first.kept, first.got, second.kept, second.got, third.kept, third.got, misc],
        smem=1,
        name="finish_rest",
    )
    return jnp.swapaxes(latent_grad, 1, 2), disco_grad_t.T, grad_expand, reduce_grad_t.T, decode_grad_t.T


def solution(mesh):
    placed = (
        P("member", None, "lon", None),
        P("member"),
        P(),
        P(),
        P(),
        P(),
        P(),
        P(),
        P(),
        P(None, "lon", None),
    )
    return jax.shard_map(
        per_device,
        mesh=mesh,
        in_specs=placed,
        out_specs=(P("member", None, "lon", None), P(), P(), P(), P()),
        check_vma=False,
    )
```

```python
import functools
import math

import jax
import jax.numpy as jnp
from jax import lax
from jax.experimental import pallas as pl
from jax.experimental.layout import Layout, with_layout_constraint
from jax.experimental.pallas import tpu as pltpu
from jax.sharding import PartitionSpec as P

reach = 3
taps = 2 * reach + 1
smooth = 0.5
LANES = 128
TILE = 16
VMEM_LIMIT = 24 * 2**20
F32 = jnp.float32
BF16 = jnp.bfloat16


def up(value, unit):
    return -(-value // unit) * unit


def dot(a, b, ca=1, cb=0):
    return lax.dot_general(a, b, (((ca,), (cb,)), ((), ())), preferred_element_type=F32)


def slope(d):
    return d * lax.rsqrt(d * d + smooth * smooth)


def vmem_call(body, outs, args, smem=0, scratch=(), name=None, moved=0):
    specs = [pl.BlockSpec(memory_space=pltpu.SMEM)] * smem
    specs += [pl.BlockSpec(memory_space=pltpu.VMEM)] * (len(args) - smem)
    return pl.pallas_call(
        body,
        out_shape=[jax.ShapeDtypeStruct(shape, dtype) for shape, dtype in outs],
        in_specs=specs,
        out_specs=[pl.BlockSpec(memory_space=pltpu.VMEM)] * len(outs),
        scratch_shapes=list(scratch),
        compiler_params=pltpu.CompilerParams(vmem_limit_bytes=VMEM_LIMIT),
        cost_estimate=pl.CostEstimate(flops=0, bytes_accessed=moved, transcendentals=0),
        name=name,
    )(*args)


def prepare_body(dims, seeds, bands, basis, table, stencil_out, offsets_out):
    members, rows, lons, chans, lon_pad, slot, bases, piece, share = dims
    points = rows * lon_pad
    per_tile = LANES // slot
    lane = lax.broadcasted_iota(jnp.int32, (lon_pad, LANES), 1)
    lon = lax.broadcasted_iota(jnp.int32, (lon_pad, LANES), 0)
    place = lane % slot
    own = place < lons
    before = (place >= lon_pad) & (place < lon_pad + reach)
    after = (place >= lon_pad + 8) & (place < lon_pad + 8 + reach)
    wide_lon = jnp.where(own, place + reach, jnp.where(before, place - lon_pad, place - lon_pad - 8 + lons + reach))
    tap = jnp.where((own | before | after) & (lon < lons), wide_lon - lon, -1)
    tap = jnp.where(lane < slot, tap, tap + 1000 * (lane // slot))
    masks = [[tap == 1000 * part + b for b in range(taps)] for part in range(per_tile)]
    for r in range(rows):
        band = bands[r]
        for k in range(bases):
            for t in range(rows // per_tile):
                block = jnp.zeros((lon_pad, LANES), F32)
                for part in range(per_tile):
                    a = t * per_tile + part - r + reach
                    if not 0 <= a < taps:
                        continue
                    base = ((band * bases + k) * taps + a) * taps
                    for b in range(taps):
                        block = jnp.where(masks[part][b], basis[base + b], block)
                stencil_out[k * points + r * lon_pad : k * points + (r + 1) * lon_pad, t * LANES : (t + 1) * LANES] = block.astype(BF16)
    seed_count = table.shape[0]
    mrow = lax.broadcasted_iota(jnp.int32, (TILE, seed_count), 0)
    mcol = lax.broadcasted_iota(jnp.int32, (TILE, seed_count), 1)
    onehot = jnp.zeros((TILE, seed_count), F32)
    for m in range(members):
        onehot = jnp.where((mrow == m) & (mcol == seeds[m]), 1.0, onehot)
    offsets_out[...] = dot(onehot.astype(BF16), table[...])


def forward_body(
    dims, place, latent, left, right, stencil, offsets_in, w_disco, w_expand, *refs
):
    members, rows, lons, chans, lon_pad, slot, bases, piece, share = dims
    spread_out, hidden_out, gelu_out, pre_out, wide = refs
    chan_pad = up(chans, LANES)
    points = rows * lon_pad
    offsets = offsets_in[...]
    wide[...] = jnp.zeros_like(wide)
    for m in range(members):
        off = offsets[m : m + 1, :]
        for r in range(rows):
            for ref, start, count in ((latent, 0, lons), (left, lon_pad, reach), (right, lon_pad + 8, reach)):
                seeded = (ref[m, r].astype(F32) + off).astype(BF16).astype(F32)
                wide[m, r * slot + start : r * slot + start + count, :chans] = seeded
    for m in range(members):
        full = wide[m]
        carry = None
        for k in range(bases):
            moved = full if k == 0 else pltpu.roll(full, k, 1)
            out = dot(stencil[k * points : (k + 1) * points, :], moved.astype(BF16))
            width = chan_pad - LANES
            first = out[:, :LANES] if carry is None else out[:, :LANES] + carry
            rows_here = slice(m * points, (m + 1) * points)
            spread_out[rows_here, k * width : k * width + LANES] = first.astype(BF16)
            spread_out[rows_here, k * width + LANES : (k + 1) * width] = out[:, LANES:width].astype(BF16)
            carry = out[:, width:]
        spread_out[rows_here, bases * width : bases * width + LANES] = carry.astype(BF16)
    seeded_rows = jnp.concatenate(
        [wide[m, r * slot : r * slot + lon_pad, :chans] for m in range(members) for r in range(rows)], axis=0
    )
    conv = dot(spread_out[:, : bases * chans], w_disco[...], 1, 1)
    hidden = (seeded_rows + conv).astype(BF16)
    hidden_out[...] = hidden
    pre = dot(hidden, w_expand[...])
    rate = math.sqrt(2.0 / math.pi)
    square = pre * pre
    th = jnp.tanh(rate * (pre + 0.044715 * (square * pre)))
    half = 0.5 * (1.0 + th)
    act = (pre * half).astype(BF16)
    gelu_out[...] = act
    pre_out[...] = pre


def fields_body(dims, place, hidden_in, act, w_reduce, w_decode, *refs):
    members, rows, lons, chans, lon_pad, slot, bases, piece, share = dims
    mixed_out, fields_out, turned_fields = refs[0], refs[1 : 1 + share], refs[1 + share]
    hidden = hidden_in[...]
    mixed = (hidden.astype(F32) + dot(act[...], w_reduce[...], 1, 1)).astype(BF16)
    mixed_out[...] = mixed
    turned = dot(w_decode[...], mixed, 1, 1).astype(BF16)
    outs = turned.shape[0]
    if share * piece > outs:
        turned = jnp.concatenate([turned, jnp.zeros((share * piece - outs, turned.shape[1]), BF16)], axis=0)
    turned_fields[...] = turned
    for d in range(share):
        fields_out[d][...] = turned_fields[pl.ds(pl.multiple_of((place[0] ^ d) * piece, TILE), piece), :]


def slopes_body(pre_in, hidden, slope_out, hidden_turned):
    rate = math.sqrt(2.0 / math.pi)
    pre = pre_in[...]
    square = pre * pre
    th = jnp.tanh(rate * (pre + 0.044715 * (square * pre)))
    half = 0.5 * (1.0 + th)
    slope_out[...] = (half + 0.5 * pre * (1.0 - th * th) * (rate * (1.0 + 3 * 0.044715 * square))).astype(BF16)
    hidden_turned[...] = turn(hidden[...])


def crps_body(count, points, members, total, *refs):
    fields = [ref[...].astype(F32) for ref in refs[:count]]
    observed = refs[count][...].astype(F32)
    outs = refs[count + 1 :]
    turned = [[f] + [pltpu.roll(f, t * points, 1) for t in range(1, members)] for f in fields]
    for i in range(count):
        paired = jnp.zeros_like(observed)
        for j in range(count):
            for t in range(members):
                if i == j and t == 0:
                    continue
                paired = paired + slope(fields[i] - turned[j][t])
        outs[i][...] = (slope(fields[i] - observed) - paired * (1.0 / (total - 1))).astype(BF16)


def turn(x):
    n, c = x.shape
    wide = jnp.concatenate([x.astype(F32), jnp.zeros((n, up(c, LANES) - c), F32)], axis=1)
    return jnp.swapaxes(wide, 0, 1)[: up(c, TILE)].astype(BF16)


def misc_rows(count, width):
    return -(-count // width), count - count // width * width


def fold_rows(rows, width, first, into):
    n = rows.shape[1]
    count = -(-n // width)
    if count * width > n:
        rows = jnp.concatenate([rows, jnp.zeros((1, count * width - n), rows.dtype)], axis=1)
    at = lax.broadcasted_iota(jnp.int32, into.shape, 0)
    for t in range(count):
        into = jnp.where(at == first + t, rows[:, t * width : (t + 1) * width], into)
    return into, first + count


def fold_ends(left_turned, left, right, width, at, misc):
    count = right.shape[1]
    last = dot(left_turned[width:], right)
    misc, at = fold_rows(last[0:1], width, at, misc)
    rest = count // width * width
    lanes = dot(turn(right[:, rest:])[:TILE], left[:, :width])
    for i in range(count - rest):
        misc, at = fold_rows(lanes[i : i + 1], width, at, misc)
    return misc, at


class Halves:
    def __init__(self, bit, keep, send):
        self.bit, self.keep, self.send = bit, keep, send
        self.half = keep.shape[0]

    def put(self, row, value):
        value = value.astype(BF16)
        for side in (0, 1):
            low, high = max(row, side * self.half), min(row + value.shape[0], (side + 1) * self.half)
            if low >= high:
                continue
            part = value[low - row : high - row]
            at = slice(low - side * self.half, high - side * self.half)

            @pl.when(self.bit == side)
            def _():
                self.keep[at, :] = part

            @pl.when(self.bit != side)
            def _():
                self.send[at, :] = part

    def zero_from(self, row):
        count = 2 * self.half - row
        if count:
            self.put(row, jnp.zeros((count, self.keep.shape[1]), F32))


def first_body(dims, scale, place, *refs):
    share, piece, outs, hidden_units, width = dims
    grads = refs[:share]
    w_decode, gelu, mixed, keep, send, mixed_grad_out, mixed_turned, field_out, turned_grad = refs[share:]
    for d in range(share):
        turned_grad[pl.ds(pl.multiple_of((place[0] ^ d) * piece, TILE), piece), :] = grads[d][...]
    field_t = turned_grad[: up(outs, TILE)]
    field_out[...] = field_t
    packed = Halves(place[1], keep, send)
    field = jnp.swapaxes(field_t.astype(F32), 0, 1).astype(BF16)[:, :outs]
    mixed_grad = dot(field, w_decode[...]).astype(BF16)
    mixed_grad_out[...] = mixed_grad
    mixed_grad_t = turn(mixed_grad)
    mixed_turned[...] = mixed_grad_t
    row = 0
    for part in range(hidden_units // width):
        packed.put(row, dot(mixed_grad_t[:width], gelu[:, part * width : (part + 1) * width]) * scale)
        row += width
    decode_grad = dot(field_t[:outs], mixed[:, :width]) * scale
    if up(outs, TILE) > outs:
        decode_grad = jnp.concatenate([decode_grad, jnp.zeros((up(outs, TILE) - outs, width), F32)], axis=0)
    packed.put(row, decode_grad)
    packed.zero_from(row + up(outs, TILE))


def second_body(dims, scale, place, *refs):
    outs, chans, hidden_units, width, taps_count = dims
    (
        mixed_grad_in, mixed_turned, field_t, w_reduce, w_expand, slopes, hidden, hidden_turned_in, gelu, mixed, spread,
        keep, send, hidden_grad_out, hidden_turned,
    ) = refs
    packed = Halves(place[1], keep, send)
    mixed_grad = mixed_grad_in[...]
    gelu_grad = dot(mixed_grad, w_reduce[...])
    pre_grad = (gelu_grad * slopes[...].astype(F32)).astype(BF16)
    hidden_grad = (mixed_grad.astype(F32) + dot(pre_grad, w_expand[...], 1, 1)).astype(BF16)
    hidden_grad_out[...] = hidden_grad
    hidden_grad_t = turn(hidden_grad)
    hidden_turned[...] = hidden_grad_t
    hidden_t = hidden_turned_in[...]
    row = 0
    for part in range(hidden_units // width):
        packed.put(row, dot(hidden_t[:width], pre_grad[:, part * width : (part + 1) * width]) * scale)
        row += width
    packed.put(row, dot(hidden_grad_t[:width], spread[:, :width]) * scale)
    row += width
    misc = jnp.zeros((misc_height(chans, hidden_units, outs, taps_count, width), width), F32)
    misc, at = fold_ends(hidden_t, hidden[...], pre_grad, width, 0, misc)
    misc, at = fold_ends(mixed_turned[...], mixed_grad, gelu[...], width, at, misc)
    misc, at = fold_ends(hidden_grad_t, hidden_grad, spread[:, :taps_count], width, at, misc)
    tail = dot(turn(mixed[:, width:])[:TILE], field_t[:outs], 1, 1)
    misc, at = fold_rows(tail[0:1], width, at, misc)
    packed.put(row, misc * scale)
    packed.zero_from(row + misc.shape[0])


def misc_height(chans, hidden_units, outs, taps_count, width):
    return up(2 * sum(misc_rows(hidden_units, width)) + sum(misc_rows(taps_count, width)) + 1, TILE)


def third_body(scale, width, place, left, right, keep, send):
    packed = Halves(place[1], keep, send)
    row = 0
    while row < keep.shape[0] * 2 // width * width:
        at = row + width
        packed.put(row, dot(left[:width, :], right[:, at : at + width]) * scale)
        row += width
    packed.zero_from(row)


def bit_of(place, pair):
    return jnp.where(place[1] == 0, place[pair[0]], place[pair[1]])


def combine_body(pair, place, kept, got, send, keep):
    count = keep.shape[0]
    bit = bit_of(place, pair)
    for target, side in ((send, 1 - bit), (keep, bit)):
        rows = pl.ds(pl.multiple_of(side * count, TILE), count)
        target[...] = add_rounded(kept[rows, :], got[rows, :])


class Joined:
    def __init__(self, bit, kept, got):
        self.bit, self.halves = bit, (kept, got)
        self.half = kept.shape[0]

    def parts(self, row, count):
        for side in (0, 1):
            low, high = max(row, side * self.half), min(row + count, (side + 1) * self.half)
            if low < high:
                kept, got = (ref[low - side * self.half : high - side * self.half, :] for ref in self.halves)
                yield low - row, jnp.where(self.bit == side, kept, got)


def put_matrix(out, block_of, misc, at, width):
    count = out.shape[1]
    for part in range(count // width):
        source, row = block_of(part)
        for offset, value in source.parts(row, width):
            out[offset : offset + value.shape[0], part * width : (part + 1) * width] = value
    wide, lanes = misc_rows(count, width)
    rest = count // width * width
    if lanes:
        ends = jnp.swapaxes(misc[at + wide : at + wide + lanes], 0, 1)
        out[:width, rest:] = ends.astype(BF16)
    for t in range(wide):
        size = min(width, count - t * width)
        out[width : width + 1, t * width : t * width + size] = misc[at + t : at + t + 1, :size].astype(BF16)
    return at + wide + lanes


def finish_second_body(dims, place, kept, got, expand_out, misc_out):
    hidden_units, width = dims
    source = Joined(place[1], kept, got)
    for offset, value in source.parts((hidden_units // width + 1) * width, misc_out.shape[0]):
        misc_out[offset : offset + value.shape[0], :] = value
    put_matrix(expand_out, lambda part: (source, part * width), misc_out[...].astype(F32), 0, width)


def finish_rest_body(dims, place, kept, got, kept_second, got_second, kept_third, got_third, misc_ref, reduce_out, decode_out, disco_out):
    hidden_units, outs, taps_count, width = dims
    first, second = Joined(place[1], kept, got), Joined(place[1], kept_second, got_second)
    third = Joined(place[1], kept_third, got_third)
    misc = misc_ref[...].astype(F32)
    base = hidden_units // width * width
    at = sum(misc_rows(hidden_units, width))
    at = put_matrix(reduce_out, lambda part: (first, part * width), misc, at, width)
    at = put_matrix(disco_out, lambda part: (third, (part - 1) * width) if part else (second, base), misc, at, width)
    for offset, value in first.parts(base, outs):
        decode_out[offset : offset + value.shape[0], :width] = value
    turned = jnp.swapaxes(misc[at : at + 8], 0, 1)
    decode_out[:, width:] = turned[:outs, : decode_out.shape[1] - width].astype(BF16)


def collect_body(dims, hidden_grad, w_disco, stencil, out, left_out, right_out):
    members, rows, lons, chans, lon_pad, slot, bases = dims
    chan_pad = up(chans, LANES)
    points = rows * lon_pad
    width = chan_pad - LANES
    full = bases * width + LANES
    grad = dot(hidden_grad[...], w_disco[...]).astype(BF16)
    grad = jnp.concatenate([grad, jnp.zeros((grad.shape[0], full - grad.shape[1]), BF16)], axis=1)
    for m in range(members):
        total = None
        for k in range(bases):
            part = dot(stencil[k * points : (k + 1) * points, :], grad[m * points : (m + 1) * points, k * width : k * width + chan_pad], 0, 0)
            part = part if k == 0 else pltpu.roll(part, chan_pad - k, 1)
            total = part if total is None else total + part
        for r in range(rows):
            at = r * slot
            own = hidden_grad[m * points + r * lon_pad : m * points + (r + 1) * lon_pad, :].astype(F32)
            out[m, r] = (own + total[at : at + lon_pad, :chans])[:lons]
            left_out[m, r] = total[at + lon_pad : at + lon_pad + 8, :chans][:reach]
            right_out[m, r] = total[at + lon_pad + 8 : at + lon_pad + 16, :chans][:reach]


def bits_of(axis):
    size, out, bit = lax.axis_size(axis), [], 1
    while bit < size:
        out.append((axis, bit))
        bit *= 2
    return out


def swap(x, pair):
    members, lons = lax.axis_size("member"), lax.axis_size("lon")
    perm = []
    for m in range(members):
        for n in range(lons):
            axis, bit = pair[n % 2]
            to = (m ^ bit) * lons + n if axis == "member" else m * lons + (n ^ bit)
            perm.append((m * lons + n, to))
    return lax.ppermute(x, ("member", "lon"), perm)


def add_rounded(a, b):
    return (a.astype(F32) + b.astype(F32)).astype(BF16)


def streams():
    core, *lon = [(d, d) for d in bits_of("lon")]
    mem = bits_of("member")
    mem = [(d, d) for d in mem]
    orders = [[mem[0], lon[0], lon[1], mem[1]], [lon[0], lon[1], mem[0], mem[1]], [lon[1], mem[0], lon[0], mem[1]]]
    return [[core] + order for order in orders]


def row_unit():
    return 8 * 2 ** (len(streams()[0]) - 1)


def all_dims():
    return bits_of("lon") + bits_of("member")


def places_of(pair):
    return [1 + all_dims().index(dim) for dim in pair]


class Stream:
    def __init__(self, place, keep, send, order):
        self.place, self.kept, self.order = place, keep, order
        self.got = swap(send, order[0])
        self.done = [order[0]]
        self.steps = [self.halve] * (len(order) - 2) + [self.exchange, self.added] + [self.join] * (len(order) - 2)

    def advance(self, last=None):
        if last is not None and last is not self:
            self.got, last.kept = lax.optimization_barrier((self.got, last.kept))
        self.steps.pop(0)()
        return self

    def halve(self):
        pair = self.order[len(self.done)]
        count, at = self.kept.shape[0] // 2, places_of(pair)
        if count % TILE == 0 and len(self.done) < 3:
            shape = ((count, self.kept.shape[1]), BF16)
            args = [self.place, self.kept, self.got]
            send, keep = vmem_call(functools.partial(combine_body, at), [shape] * 2, args, smem=1, name="combine")
        else:
            bit = bit_of(self.place, at)
            send, keep = (
                add_rounded(*(lax.dynamic_slice_in_dim(x, side * count, count, axis=0) for x in (self.kept, self.got)))
                for side in (1 - bit, bit)
            )
        self.got, self.kept = swap(send, pair), keep
        self.done.append(pair)

    def exchange(self):
        self.kept = add_rounded(self.kept, self.got)
        self.got = swap(self.kept, self.order[-1])

    def added(self):
        self.kept = add_rounded(self.kept, self.got)
        self.send_back()

    def join(self):
        low = bit_of(self.place, places_of(self.done.pop())) == 0
        self.kept = jnp.concatenate([jnp.where(low, self.kept, self.got), jnp.where(low, self.got, self.kept)], axis=0)
        self.send_back()

    def send_back(self):
        self.got = swap(self.kept, self.done[-1])


def shifted(x, axis, by):
    size = lax.axis_size(axis)
    return lax.ppermute(x, axis, [(i, (i + by) % size) for i in range(size)])


def exchanged(piece_of, axis):
    size = lax.axis_size(axis)
    return [piece_of(0)] + [lax.ppermute(piece_of(d), axis, [(i, i ^ d) for i in range(size)]) for d in range(1, size)]


def per_device(
    latent, member_seeds, member_table, row_bands, disco_basis, w_disco, w_expand, w_reduce, w_decode, target
):
    members, rows, lons, chans = latent.shape
    bases = disco_basis.shape[1]
    hidden_units = w_expand.shape[1]
    outs = w_decode.shape[1]
    share = lax.axis_size("member")
    total_members = members * share
    lon_pad = up(lons, TILE)
    slot = lon_pad + TILE
    points = rows * lon_pad
    flat = members * points
    width = chans // LANES * LANES
    full = bases * width + LANES
    piece = TILE * -(-up(outs, TILE) // (TILE * share))
    me = lax.axis_index("member")
    place = jnp.stack([me] + [lax.axis_index(axis) // bit % 2 for axis, bit in all_dims()]).astype(jnp.int32)
    by_lon = jnp.swapaxes(latent, 1, 2)
    left = jnp.swapaxes(shifted(by_lon[:, lons - reach :], "lon", 1), 1, 2)
    right = jnp.swapaxes(shifted(by_lon[:, :reach], "lon", -1), 1, 2)
    disco_t, reduce_t, decode_t = w_disco.T, w_reduce.T, w_decode.T
    dims = (members, rows, lons, chans, lon_pad, slot, bases, piece, share)
    stencil, offsets = vmem_call(
        functools.partial(prepare_body, dims),
        [((bases * points, rows * slot), BF16), ((TILE, chans), F32)],
        [member_seeds, row_bands, disco_basis.astype(F32).reshape(-1), member_table],
        smem=3,
        name="prepare",
        moved=4 * 2**20,
    )
    spread, hidden, gelu, pre = vmem_call(
        functools.partial(forward_body, dims),
        [((flat, full), BF16), ((flat, chans), BF16), ((flat, hidden_units), BF16), ((flat, hidden_units), F32)],
        [place, latent, left, right, stencil, offsets, disco_t, w_expand],
        smem=1,
        scratch=[pltpu.VMEM((members, rows * slot, up(chans, LANES)), F32)],
        name="forward",
        moved=24 * 2**20,
    )
    mixed, *here = vmem_call(
        functools.partial(fields_body, dims),
        [((flat, chans), BF16)] + [((piece, flat), BF16)] * share,
        [place, hidden, gelu, reduce_t, decode_t],
        smem=1,
        scratch=[pltpu.VMEM((share * piece, flat), BF16)],
        name="fields",
        moved=6 * 2**20,
    )
    turned_shape = ((up(chans, TILE), flat), BF16)
    slopes, input_turned = vmem_call(
        slopes_body, [((flat, hidden_units), BF16), turned_shape], [pre, hidden], name="slopes"
    )
    here_out = here
    observed = jnp.pad(target, ((0, 0), (0, lon_pad - lons), (0, share * piece - outs))).reshape(points, share * piece).T
    observed = jnp.concatenate([observed] * members, axis=1)
    observed = lax.dynamic_slice_in_dim(observed, me * piece, piece, axis=0)
    here = exchanged(lambda d: here_out[d], "member")
    observed, slopes, input_turned = lax.optimization_barrier((observed, slopes, input_turned))
    grads = vmem_call(
        functools.partial(crps_body, share, points, members, total_members),
        [((piece, flat), BF16)] * share,
        here + [observed],
        name="crps",
        moved=3 * 2**20,
    )
    back = exchanged(lambda d: grads[d], "member")
    scale = 1.0 / math.sqrt(total_members * rows * lons * lax.axis_size("lon"))
    unit = row_unit()
    taps_count = bases * chans
    orders = streams()

    def halves(rows):
        return [((up(rows, unit) // 2, width), BF16)] * 2

    blocks = hidden_units // width
    keep, send, mixed_grad, mixed_turned, field_turned = vmem_call(
        functools.partial(first_body, (share, piece, outs, hidden_units, width), scale),
        halves(blocks * width + up(outs, TILE)) + [((flat, chans), BF16), turned_shape, ((up(outs, TILE), flat), BF16)],
        [place] + back + [decode_t, gelu, mixed],
        smem=1,
        scratch=[pltpu.VMEM((share * piece, flat), BF16)],
        name="first_products",
        moved=9 * 2**20,
    )
    first = Stream(place, keep, send, orders[0])
    misc_shape = ((misc_height(chans, hidden_units, outs, taps_count, width), width), BF16)
    keep, send, hidden_grad, hidden_turned = vmem_call(
        functools.partial(second_body, (outs, chans, hidden_units, width, taps_count), scale),
        halves((blocks + 1) * width + misc_shape[0][0]) + [((flat, chans), BF16), turned_shape],
        [place, mixed_grad, mixed_turned, field_turned, reduce_t, w_expand, slopes, hidden, input_turned, gelu, mixed, spread],
        smem=1,
        name="second_products",
    )
    second = Stream(place, keep, send, orders[1])
    first.advance()
    hidden_turned, first.kept = lax.optimization_barrier((hidden_turned, first.kept))
    keep, send = vmem_call(
        functools.partial(third_body, scale, width),
        halves((taps_count // width - 1) * width),
        [place, hidden_turned, spread],
        smem=1,
        name="third_products",
    )
    third = Stream(place, keep, send, orders[2])
    second.advance()
    last = third.advance(second)
    hidden_grad, third.kept = lax.optimization_barrier((hidden_grad, third.kept))
    dims = (members, rows, lons, chans, lon_pad, slot, bases)
    latent_grad, to_left, to_right = vmem_call(
        functools.partial(collect_body, dims),
        [(latent.shape, F32), ((members, rows, reach, chans), F32), ((members, rows, reach, chans), F32)],
        [hidden_grad, disco_t, stencil],
        name="collect",
    )
    first.got, latent_grad = lax.optimization_barrier((first.got, latent_grad))
    from_right = shifted(to_left, "lon", -1)
    from_left = shifted(to_right, "lon", 1)
    for stream in (first, second, third) * 4:
        last = stream.advance(last)
    first.got, from_right, from_left = lax.optimization_barrier((first.got, from_right, from_left))
    edge = [(0, 0, 0)] * 2
    latent_grad = (
        latent_grad
        + lax.pad(from_right, jnp.float32(0), edge + [(lons - reach, 0, 0), (0, 0, 0)])
        + lax.pad(from_left, jnp.float32(0), edge + [(0, lons - reach, 0), (0, 0, 0)])
    ).astype(BF16)

    latent_grad = with_layout_constraint(jnp.swapaxes(latent_grad, 1, 2), Layout(major_to_minor=(0, 1, 2, 3)))
    for stream in (first, second, third):
        last = stream.advance(last)
    first.got, latent_grad = lax.optimization_barrier((first.got, latent_grad))
    while third.steps:
        for stream in (second, first, third):
            if stream.steps:
                last = stream.advance(last)
    grad_expand, misc = vmem_call(
        functools.partial(finish_second_body, (hidden_units, width)),
        [(w_expand.shape, BF16), misc_shape],
        [place, second.kept, second.got],
        smem=1,
        name="finish_second",
    )
    reduce_grad_t, decode_grad_t, disco_grad_t = vmem_call(
        functools.partial(finish_rest_body, (hidden_units, outs, taps_count, width)),
        [(reduce_t.shape, BF16), (decode_t.shape, BF16), (disco_t.shape, BF16)],
        [place, first.kept, first.got, second.kept, second.got, third.kept, third.got, misc],
        smem=1,
        name="finish_rest",
    )
    return jnp.swapaxes(latent_grad, 1, 2), disco_grad_t.T, grad_expand, reduce_grad_t.T, decode_grad_t.T


def solution(mesh):
    placed = (
        P("member", None, "lon", None),
        P("member"),
        P(),
        P(),
        P(),
        P(),
        P(),
        P(),
        P(),
        P(None, "lon", None),
    )
    return jax.shard_map(
        per_device,
        mesh=mesh,
        in_specs=placed,
        out_specs=(P("member", None, "lon", None), P(), P(), P(), P()),
        check_vma=False,
    )
```
